128 devices in a mesh: grid: 8 (over z, core), mesh: 16 (over x, y).
Axes of the slice: x: 4, y: 4, z: 4, core: 2. Of those that a mesh axis runs over, the one named last changes fastest.
Arguments:
- grid_latent: bfloat16 [393216, 512], P(('grid', 'mesh')), may hold values from -6 to 6
- mesh_latent: bfloat16 [32768, 512], P('mesh'), may hold values from -6 to 6
- mesh_cotangent: bfloat16 [32768, 512], P('mesh'), may hold values from -18 to 18
- w_send: bfloat16 [512, 512], replicated, may hold values from -0.25 to 0.25
- w_self_enc: bfloat16 [512, 512], replicated, may hold values from -0.25 to 0.25
- w_agg_enc: bfloat16 [512, 512], replicated, may hold values from -0.0078125 to 0.0078125
- w_out_enc: bfloat16 [512, 512], replicated, may hold values from -0.25 to 0.25
- w_pass: bfloat16 [512, 512], replicated, may hold values from -0.25 to 0.25
- w_self_proc: bfloat16 [512, 512], replicated, may hold values from -0.25 to 0.25
- w_agg_proc: bfloat16 [512, 512], replicated, may hold values from -0.01171875 to 0.01171875
- w_out_proc: bfloat16 [512, 512], replicated, may hold values from -0.25 to 0.25
- enc_source: int32 [4096], P(('grid', 'mesh')), may hold values from 0 to 23
- enc_part: int32 [4096, 1], P(('grid', 'mesh')), may hold values from 0 to 15; in each aligned block of 32 rows (0 to 31, 32 to 63, ...) at most 3 rows name the same one
- enc_block: int32 [4096], P(('grid', 'mesh')), may hold values from 0 to 15
- enc_mask: int32 [4096, 128, 128], P(('grid', 'mesh')), may hold values 0 or 1
- proc_source: int32 [2048], P(('grid', 'mesh')), may hold values from 0 to 47
- proc_target: int32 [2048], P(('grid', 'mesh')), may hold values from 0 to 15
- proc_mask: int32 [2048, 128, 128], P(('grid', 'mesh')), may hold values 0 or 1
Outputs:
- mesh_out: bfloat16 [32768, 512], P('mesh')
- grid_grad: bfloat16 [393216, 512], P(('grid', 'mesh'))
The draws below stay inside these ranges and needn't reach their ends.
Inputs may be any that keep to these rules, and one draw needn't show every extreme that they name: `enc_part`: within the rows of one device, no partition is named by more than 3 rows.
All inputs are finite; a program needn't handle non-finite values. No bound on the sum of `enc_mask` or of `proc_mask` on one device may be relied on, other than what follows from the above.
Results may differ from the reference program's by a relative error of at most 0.033.
Values may be sent and summed in bfloat16 or wider, within the bound.
No kernel may reach another device: no remote copies, remote signals or barrier semaphores. Data moves between devices by JAX's collectives and lax.ppermute only.
A program may use at most 192 MiB of HBM per device.

```python
import math
import jax
import jax.numpy as jnp
import numpy as np
from jax import lax

D = 512
BLK = 128
GB_DEV = 24
MB_DEV = 16
EB_DEV = 32
ME_DEV = 16
CAP = 3
NGRID = 393216
NMESH = 32768
N_GRID = 8
N_MESH = 16
DEVICES = 128


def with_ends(values, key, smallest, top_value):
    index_at = [jax.random.randint(jax.random.fold_in(key, axis), (), 0, length) for axis, length in enumerate(values.shape)]
    main_axis = values.shape.index(max(values.shape))
    neighbour = index_at[:main_axis] + [(index_at[main_axis] + 1) % values.shape[main_axis]] + index_at[main_axis + 1:]
    return values.at[tuple(index_at)].set(smallest).at[tuple(neighbour)].set(top_value)


def steps_of(rng, dims, split, least, largest):
    def one(axis_at, parts):
        steps = jax.random.uniform(jax.random.fold_in(jax.random.fold_in(rng, 6), axis_at), (parts,), jnp.float32, least / len(split), largest / len(split))
        return jnp.repeat(jnp.exp(steps), dims[axis_at] // parts).reshape((-1,) + (1,) * (len(dims) - axis_at - 1))

    gain = one(*split[0])
    for cut in split[1:]:
        gain = gain * one(*cut)
    return gain


def routed_block(stream_key, own, number, rows, number_of, top, most, skew):
    sequence = jax.random.permutation(stream_key, number_of)
    crowded, common = load_shares(number_of, rows * top, most, skew, True), load_shares(number_of, rows * top, most, skew, False)
    places = jnp.arange(number_of)

    def named(sizes, turn):
        used = int((sizes > 0).sum())
        fixed = max(1, used // 4)
        moved = fixed + (places - fixed + turn * (used - fixed)) % max(1, number_of - fixed)
        return jnp.zeros((number_of,), jnp.int32).at[sequence[jnp.where(places < fixed, places, moved)]].set(jnp.asarray(sizes, jnp.int32))

    sizes = jnp.where(number % 4 == 0, named(crowded, number // 4), named(common, number - number // 4 - 1))
    mixed = jax.random.permutation(jax.random.fold_in(own, 3), number_of)
    source_of, receiver = mixed[0:number_of // 2 * 2:2], mixed[1:number_of // 2 * 2:2]
    slack = jnp.minimum(sizes[source_of] - 1, most - sizes[receiver]) // 2
    slack = jnp.where((source_of == sequence[0]) | (receiver == sequence[0]) | (sizes[receiver] == 0), 0, jnp.maximum(slack, 0))
    moved = jax.random.randint(jax.random.fold_in(own, 4), (number_of // 2,), 0, 1 << 20) % (slack + 1)
    sizes = sizes.at[source_of].add(-moved).at[receiver].add(moved)
    labels = jnp.searchsorted(jnp.cumsum(sizes), jnp.arange(rows * top), side="right").astype(jnp.int32)
    grid = labels.reshape(top, rows).T
    grid = grid[jax.random.permutation(jax.random.fold_in(own, 1), rows)]
    turn = jax.random.randint(jax.random.fold_in(own, 2), (rows, 1), 0, top)
    return jnp.take_along_axis(grid, (jnp.arange(top)[None, :] + turn) % top, axis=1)


def load_shares(number_of, total, limit, lean, full):
    portions = [(1 << 20) // math.isqrt(grade ** lean) + 1 for grade in range(1, number_of + 1)]
    largest = limit if full else min(limit, max(-(-total // number_of), total * portions[0] // sum(portions)))
    least = 1 if total - largest >= number_of - 1 else 0
    counts, spare = [largest] + [least] * (number_of - 1), total - largest - least * (number_of - 1)
    while spare > 0:
        movable = [i for i in range(1, number_of) if counts[i] < largest] or [i for i in range(1, number_of) if counts[i] < limit]
        mass, budget = sum([portions[i] for i in movable]), spare
        for i in movable:
            more = min(limit - counts[i], max(1, budget * portions[i] // mass), spare)
            counts[i] = counts[i] + more
            spare = spare - more
    return np.array(counts)


def noise(stream_key, dims, deviation, bound, split=(), held_as=jnp.bfloat16):
    level = steps_of(stream_key, dims, split, -0.22, 0.18) if split else 1.0
    values = jax.random.normal(stream_key, dims, jnp.float32) * deviation * level
    return jnp.minimum(jnp.maximum(values, -bound), bound).astype(held_as)


def setup_inputs(seed: int = 0) -> dict:
    key_list = jax.random.split(jax.random.key(seed), 19)
    grid_latent = noise(key_list[0], (NGRID, D), 1.0, 6.0, ((0, 128),))
    mesh_latent = noise(key_list[1], (NMESH, D), 1.0, 6.0, ((0, 16),))
    mesh_cotangent = noise(key_list[2], (NMESH, D), 3.0, 18.0, ((0, 16),))
    w_send = noise(key_list[3], (D, D), D ** -0.5, 0.25)
    w_self_enc = noise(key_list[4], (D, D), D ** -0.5, 0.25)
    w_agg_enc = noise(key_list[5], (D, D), (D * BLK * EB_DEV * N_GRID // (2 * MB_DEV)) ** -0.5, 0.0078125)
    w_out_enc = noise(key_list[6], (D, D), D ** -0.5, 0.25)
    w_pass = noise(key_list[7], (D, D), D ** -0.5, 0.25)
    w_self_proc = noise(key_list[8], (D, D), D ** -0.5, 0.25)
    w_agg_proc = noise(key_list[9], (D, D), (D * BLK * ME_DEV * N_GRID // (2 * MB_DEV)) ** -0.5, 0.01171875)
    w_out_proc = noise(key_list[10], (D, D), D ** -0.5, 0.25)
    enc_source = with_ends(jax.random.randint(key_list[11], (DEVICES * EB_DEV,), 0, GB_DEV), jax.random.fold_in(key_list[11], 1), 0, GB_DEV - 1).astype(jnp.int32)
    enc_part_keys = jax.random.split(jax.random.fold_in(key_list[12], 1), (DEVICES * EB_DEV) // EB_DEV)
    enc_part_turns = jax.random.permutation(jax.random.fold_in(key_list[12], 3), (DEVICES * EB_DEV) // EB_DEV)
    enc_part = jax.vmap(lambda own, number: routed_block(jax.random.fold_in(key_list[12], 2), own, number, EB_DEV, N_MESH, 1, CAP, 2))(enc_part_keys, enc_part_turns).reshape((DEVICES * EB_DEV, 1))
    enc_block = with_ends(jax.random.randint(key_list[13], (DEVICES * EB_DEV,), 0, MB_DEV), jax.random.fold_in(key_list[13], 1), 0, MB_DEV - 1).astype(jnp.int32)
    enc_mask = with_ends((jax.random.randint(key_list[14], (DEVICES * EB_DEV, BLK, BLK), 0, 2) < 1).astype(jnp.int32), jax.random.fold_in(key_list[14], 1), 0, 1)
    proc_source = with_ends(jax.random.randint(key_list[15], (DEVICES * ME_DEV,), 0, 3 * MB_DEV), jax.random.fold_in(key_list[15], 1), 0, (3 * MB_DEV) - 1).astype(jnp.int32)
    proc_target = with_ends(jax.random.randint(key_list[16], (DEVICES * ME_DEV,), 0, MB_DEV), jax.random.fold_in(key_list[16], 1), 0, MB_DEV - 1).astype(jnp.int32)
    proc_mask = with_ends((jax.random.randint(key_list[17], (DEVICES * ME_DEV, BLK, BLK), 0, 2) < 1).astype(jnp.int32), jax.random.fold_in(key_list[17], 1), 0, 1)
    return {"grid_latent": grid_latent, "mesh_latent": mesh_latent, "mesh_cotangent": mesh_cotangent, "w_send": w_send, "w_self_enc": w_self_enc, "w_agg_enc": w_agg_enc, "w_out_enc": w_out_enc, "w_pass": w_pass, "w_self_proc": w_self_proc, "w_agg_proc": w_agg_proc, "w_out_proc": w_out_proc, "enc_source": enc_source, "enc_part": enc_part, "enc_block": enc_block, "enc_mask": enc_mask, "proc_source": proc_source, "proc_target": proc_target, "proc_mask": proc_mask}


def silu_slope(values):
    sigmoid_v = jax.nn.sigmoid(values)
    return sigmoid_v * (1.0 + values * (1.0 - sigmoid_v))


def settle(values):
    return lax.optimization_barrier(values.astype(jnp.bfloat16)).astype(jnp.float32)


def mesh_mlp(node_rows, summed, w_self, w_agg, w_out):
    summed_b = summed.astype(jnp.bfloat16)
    pre_act = jnp.dot(node_rows, w_self, preferred_element_type=jnp.float32) + jnp.dot(summed_b, w_agg, preferred_element_type=jnp.float32)
    hidden = jax.nn.silu(pre_act).astype(jnp.bfloat16)
    result = (node_rows.astype(jnp.float32) + jnp.dot(hidden, w_out, preferred_element_type=jnp.float32)).astype(jnp.bfloat16)
    return pre_act, result


def mlp_back(upper_grad, pre_act, w_agg, w_out):
    g_hidden = settle(jnp.dot(upper_grad, w_out.T, preferred_element_type=jnp.float32))
    g_pre = (g_hidden * silu_slope(pre_act)).astype(jnp.bfloat16)
    g_summed = jnp.dot(g_pre, w_agg.T, preferred_element_type=jnp.float32).astype(jnp.bfloat16)
    return g_pre, g_summed


def reference(grid_latent, mesh_latent, mesh_cotangent, w_send, w_self_enc, w_agg_enc, w_out_enc, w_pass, w_self_proc, w_agg_proc, w_out_proc, enc_source, enc_part, enc_block, enc_mask, proc_source, proc_target, proc_mask):
    total_blocks = N_MESH * MB_DEV
    sent_rows = jnp.dot(grid_latent, w_send, preferred_element_type=jnp.float32).astype(jnp.bfloat16)
    sent_blocks = sent_rows.reshape(DEVICES, GB_DEV, BLK, D)
    enc_src = enc_source.reshape(DEVICES, EB_DEV).astype(jnp.int32)
    enc_dst = (enc_part.reshape(DEVICES, EB_DEV) * MB_DEV + enc_block.reshape(DEVICES, EB_DEV)).astype(jnp.int32)
    enc_masks = enc_mask.reshape(DEVICES, EB_DEV, BLK, BLK)

    def enc_device(device_id):
        src_rows = jnp.take(sent_blocks[device_id], enc_src[device_id], axis=0).astype(jnp.float32)
        masks_now = enc_masks[device_id].astype(jnp.float32)
        messages = settle(jnp.einsum("eij,eid->ejd", masks_now, src_rows))
        return jax.ops.segment_sum(messages, enc_dst[device_id], num_segments=total_blocks)

    def enc_band(running, band_id):
        def add_device(inner, part_id):
            return inner + enc_device(band_id * N_MESH + part_id), None
        zero_blocks = jnp.zeros((total_blocks, BLK, D), jnp.float32)
        partial_value, _ = lax.scan(add_device, zero_blocks, jnp.arange(N_MESH, dtype=jnp.int32))
        return running + settle(partial_value), None

    agg_enc, _ = lax.scan(enc_band, jnp.zeros((total_blocks, BLK, D), jnp.float32), jnp.arange(N_GRID, dtype=jnp.int32))
    agg_enc = agg_enc.reshape(total_blocks * BLK, D)
    pre_enc, first = mesh_mlp(mesh_latent, agg_enc, w_self_enc, w_agg_enc, w_out_enc)
    passed = jnp.dot(first, w_pass, preferred_element_type=jnp.float32).astype(jnp.bfloat16)
    passed_parts = passed.reshape(N_MESH, MB_DEV, BLK, D)
    proc_src = proc_source.reshape(N_GRID, N_MESH, ME_DEV).astype(jnp.int32)
    proc_dst = proc_target.reshape(N_GRID, N_MESH, ME_DEV).astype(jnp.int32)
    proc_masks = proc_mask.reshape(N_GRID, N_MESH, ME_DEV, BLK, BLK)

    def proc_part(part_id):
        lower_id = (part_id + N_MESH - 1) % N_MESH
        upper_id = (part_id + 1) % N_MESH
        extended = jnp.concatenate([passed_parts[lower_id], passed_parts[part_id], passed_parts[upper_id]], axis=0)

        def add_band(running, band_id):
            src_rows = jnp.take(extended, proc_src[band_id, part_id], axis=0).astype(jnp.float32)
            masks_now = proc_masks[band_id, part_id].astype(jnp.float32)
            messages = jnp.einsum("eij,eid->ejd", masks_now, src_rows)
            partial_value = jax.ops.segment_sum(messages, proc_dst[band_id, part_id], num_segments=MB_DEV)
            return running + settle(partial_value), None

        running_total, _ = lax.scan(add_band, jnp.zeros((MB_DEV, BLK, D), jnp.float32), jnp.arange(N_GRID, dtype=jnp.int32))
        return running_total

    agg_proc = lax.map(proc_part, jnp.arange(N_MESH, dtype=jnp.int32)).reshape(total_blocks * BLK, D)
    pre_proc, mesh_out = mesh_mlp(first, agg_proc, w_self_proc, w_agg_proc, w_out_proc)
    g_pre_proc, g_agg_proc = mlp_back(mesh_cotangent, pre_proc, w_agg_proc, w_out_proc)
    g_first_part = mesh_cotangent.astype(jnp.float32) + jnp.dot(g_pre_proc, w_self_proc.T, preferred_element_type=jnp.float32)
    g_parts = g_agg_proc.reshape(N_MESH, MB_DEV, BLK, D)

    def back_band(running, band_id):
        def term_part(part_id):
            dst_rows = jnp.take(g_parts[part_id], proc_dst[band_id, part_id], axis=0).astype(jnp.float32)
            masks_now = proc_masks[band_id, part_id].astype(jnp.float32)
            contrib = jnp.einsum("eij,ejd->eid", masks_now, dst_rows)
            spread = jax.ops.segment_sum(contrib, proc_src[band_id, part_id], num_segments=3 * MB_DEV)
            return spread.reshape(3, MB_DEV, BLK, D).astype(jnp.bfloat16)

        terms = lax.optimization_barrier(lax.map(term_part, jnp.arange(N_MESH, dtype=jnp.int32)))
        from_upper = jnp.roll(terms[:, 0], -1, axis=0)
        from_lower = jnp.roll(terms[:, 2], 1, axis=0)
        grad_local = from_upper.astype(jnp.float32) + terms[:, 1].astype(jnp.float32) + from_lower.astype(jnp.float32)
        return running + settle(grad_local), None

    g_pass, _ = lax.scan(back_band, jnp.zeros((N_MESH, MB_DEV, BLK, D), jnp.float32), jnp.arange(N_GRID, dtype=jnp.int32))
    g_pass = g_pass.reshape(total_blocks * BLK, D)
    g_first = (g_first_part + jnp.dot(g_pass.astype(jnp.bfloat16), w_pass.T, preferred_element_type=jnp.float32)).astype(jnp.bfloat16)
    g_pre_enc, g_agg_enc = mlp_back(g_first, pre_enc, w_agg_enc, w_out_enc)
    g_blocks = g_agg_enc.reshape(total_blocks, BLK, D)

    def grid_device(device_id):
        dst_rows = jnp.take(g_blocks, enc_dst[device_id], axis=0).astype(jnp.float32)
        masks_now = enc_masks[device_id].astype(jnp.float32)
        contrib = jnp.einsum("eij,ejd->eid", masks_now, dst_rows)
        spread = jax.ops.segment_sum(contrib, enc_src[device_id], num_segments=GB_DEV).reshape(GB_DEV * BLK, D)
        return jnp.dot(spread.astype(jnp.bfloat16), w_send.T, preferred_element_type=jnp.float32).astype(jnp.bfloat16)

    grid_grad = lax.map(grid_device, jnp.arange(DEVICES, dtype=jnp.int32)).reshape(DEVICES * GB_DEV * BLK, D)
    return mesh_out, grid_grad
```

```python
import functools

import jax
import jax.numpy as jnp
from jax import lax
from jax.experimental import pallas as pl
from jax.experimental.pallas import tpu as pltpu
from jax.sharding import PartitionSpec as P

BF16 = jnp.bfloat16
F32 = jnp.float32
MIB = 1024 * 1024
SMEM = pl.BlockSpec(memory_space=pltpu.SMEM)
VMEM = pl.BlockSpec(memory_space=pltpu.VMEM)
PIECES = [(dz, dc) for dz in range(4) for dc in range(2)]


def over_z(array, by):
    return lax.ppermute(array, "grid", [(2 * z + c, 2 * ((z + by) % 4) + c) for z in range(4) for c in range(2)])


def over_column(array, dz, dc):
    return lax.ppermute(
        array, "grid", [(2 * z + c, 2 * ((z + dz) % 4) + (c ^ dc)) for z in range(4) for c in range(2)]
    )


def over_x(array, by):
    return lax.ppermute(array, "mesh", [(4 * x + y, 4 * ((x + by) % 4) + y) for x in range(4) for y in range(4)])


def over_y(array, by):
    return lax.ppermute(array, "mesh", [(4 * x + y, 4 * x + (y + by) % 4) for x in range(4) for y in range(4)])


def over_mesh(array, by):
    return lax.ppermute(array, "mesh", [(p, (p + by) % 16) for p in range(16)])


def local(body, outs, ins, smem=1, scratch=(), limit=24, cost=None):
    return pl.pallas_call(
        body,
        out_shape=[jax.ShapeDtypeStruct(shape, dtype) for shape, dtype in outs],
        in_specs=[SMEM] * smem + [VMEM] * (len(ins) - smem),
        out_specs=[VMEM] * len(outs),
        scratch_shapes=list(scratch),
        compiler_params=pltpu.CompilerParams(vmem_limit_bytes=limit * MIB),
    )(*ins)


def lanes(index):
    return pl.ds(pl.multiple_of((index & 3) * 128, 128), 128)


def dot(a, b):
    return jnp.dot(a, b, preferred_element_type=F32)


def dot_t(a, b):
    return lax.dot_general(a, b, (((1,), (1,)), ((), ())), preferred_element_type=F32)


def silu_slope(values):
    sigmoid_v = jax.nn.sigmoid(values)
    return sigmoid_v * (1.0 + values * (1.0 - sigmoid_v))


def messages_body(ids, source, latent, w_send, mask, *rest):
    outs, (sent, msg) = rest[:16], rest[16:]
    step = pl.program_id(0)
    z, c = ids[0], ids[1]

    @pl.when(step == 0)
    def _():
        def rows(i, _):
            at = pl.ds(pl.multiple_of(i * 256, 256), 256)
            sent[at, :] = dot(latent[at, :], w_send[...]).astype(BF16)
            return 0

        lax.fori_loop(0, 12, rows, 0)

    for k in range(4):
        block = source[step * 4 + k]
        rows = sent[pl.ds(pl.multiple_of(block * 128, 128), 128), :]
        weights = mask[k].astype(F32).astype(BF16)
        msg[k] = lax.dot_general(weights, rows, (((0,), (0,)), ((), ())), preferred_element_type=F32).astype(BF16)
        for h in range(2):
            for n, (dz, dc) in enumerate(PIECES):
                at = pl.ds(pl.multiple_of(64 * (c ^ dc) + 32 * h, 32), 32)
                outs[8 * h + n][k] = msg[k, at, lanes(z + dz)]


def send_messages(ids, source, latent, w_send, mask):
    whole = lambda i: (0, 0)
    return pl.pallas_call(
        messages_body,
        grid=(8,),
        out_shape=[jax.ShapeDtypeStruct((32, 32, 128), BF16)] * 16,
        in_specs=[
            SMEM,
            SMEM,
            pl.BlockSpec((3072, 512), whole, pipeline_mode=pl.Buffered(1)),
            pl.BlockSpec((512, 512), whole, pipeline_mode=pl.Buffered(1)),
            pl.BlockSpec((4, 128, 128), lambda i: (i, 0, 0)),
        ],
        out_specs=[pl.BlockSpec((4, 32, 128), lambda i: (i, 0, 0))] * 16,
        scratch_shapes=[pltpu.VMEM((3072, 512), BF16), pltpu.VMEM((4, 128, 512), BF16)],
        compiler_params=pltpu.CompilerParams(vmem_limit_bytes=24 * MIB),
    )(ids, source, latent, w_send, mask)


def combine_body(y_first, ids, meta, *rest):
    pieces, outs, acc = rest[:8], rest[8:12], rest[12]
    z, c, x, y = ids[0], ids[1], ids[2], ids[3]
    acc[...] = jnp.zeros_like(acc)
    for (dz, dc), piece in zip(PIECES, pieces):
        row = (2 * ((z - dz) & 3) + (c ^ dc)) * 64

        def add(e, _):
            slot = meta[row + e]
            acc[slot] += piece[e].astype(F32)
            return 0

        lax.fori_loop(0, 32, add, 0, unroll=4)
    for k in range(4):
        for j in range(4):
            kx, ky = (j, k) if y_first else (k, j)
            part = 4 * ((x + kx) & 3) + ((y + ky) & 3)
            outs[k][j] = acc[pl.ds(part * 16, 16)].astype(BF16)


def combine(y_first, ids, meta, pieces):
    return local(
        functools.partial(combine_body, y_first),
        [((4, 16, 32, 128), BF16)] * 4,
        [ids, meta, *pieces],
        smem=2,
        scratch=[pltpu.VMEM((256, 32, 128), F32)],
    )


def add_rows_body(a, b, c, d, *outs):
    for j in range(4):
        outs[j][...] = (
            a[j].astype(F32) + b[j].astype(F32) + c[j].astype(F32) + d[j].astype(F32)
        ).astype(BF16)


def add_rows(parts):
    return local(add_rows_body, [((16, 32, 128), BF16)] * 4, parts, smem=0)


def add_last_body(ids, *rest):
    halves, outs, acc = (rest[:4], rest[4:8]), rest[8:12], rest[12]
    z = ids[0]
    for h, half in enumerate(halves):
        total = half[0][...].astype(F32)
        for more in half[1:]:
            total += more[...].astype(F32)
        acc[:, 32 * h : 32 * h + 32, :] = total.astype(BF16)
    for k in range(4):
        outs[k][...] = acc[pl.ds(4 * ((z + k) & 3), 4)]


def add_last(ids, first_half, second_half):
    return local(
        add_last_body,
        [((4, 64, 128), BF16)] * 4,
        [ids, *first_half, *second_half],
        scratch=[pltpu.VMEM((16, 64, 128), BF16)],
    )


def to_rows(z, pieces, wide):
    for k in range(4):
        wide[:, lanes(z - k)] = pieces[k][...].reshape(256, 128)
    return wide[...]


def from_rows(z, wide, outs):
    for k in range(4):
        outs[k][...] = wide[:, lanes(z + k)].reshape(4, 64, 128)


def enc_mlp_body(ids, p0, p1, p2, p3, pre_self, rows, w_agg, w_out, w_pass, pre_ref, first_ref, *rest):
    outs, wide = rest[:4], rest[4]
    z = ids[0]
    summed = to_rows(z, (p0, p1, p2, p3), wide)
    pre = pre_self[...] + dot(summed, w_agg[...])
    pre_ref[...] = pre
    hidden = jax.nn.silu(pre).astype(BF16)
    first = (rows[...].astype(F32) + dot(hidden, w_out[...])).astype(BF16)
    first_ref[...] = first
    wide[...] = dot(first, w_pass[...]).astype(BF16)
    from_rows(z, wide, outs)


def proc_mlp_body(ids, p0, p1, p2, p3, pre_self, rows, g_hidden, w_agg, w_out, out_ref, g_pre_ref, *rest):
    outs, wide = rest[:4], rest[4]
    z = ids[0]
    summed = to_rows(z, (p0, p1, p2, p3), wide)
    pre = pre_self[...] + dot(summed, w_agg[...])
    g_pre = (g_hidden[...].astype(F32) * silu_slope(pre)).astype(BF16)
    g_pre_ref[...] = g_pre
    wide[...] = dot_t(g_pre, w_agg[...]).astype(BF16)
    from_rows(z, wide, outs)
    hidden = jax.nn.silu(pre).astype(BF16)
    out_ref[...] = (rows[...].astype(F32) + dot(hidden, w_out[...])).astype(BF16)


def enc_back_body(ids, p0, p1, p2, p3, g_part, pre, w_pass, w_out, w_agg, *rest):
    outs, wide = rest[:4], rest[4]
    z = ids[0]
    g_pass = to_rows(z, (p0, p1, p2, p3), wide)
    g_first = (g_part[...] + dot_t(g_pass, w_pass[...])).astype(BF16)
    g_hidden = dot_t(g_first, w_out[...]).astype(BF16)
    g_pre = (g_hidden.astype(F32) * silu_slope(pre[...])).astype(BF16)
    wide[...] = dot_t(g_pre, w_agg[...]).astype(BF16)
    from_rows(z, wide, outs)


ROWS = ((256, 512), BF16)
ROWS32 = ((256, 512), F32)
PIECE = ((4, 64, 128), BF16)
WIDE = pltpu.VMEM((256, 512), BF16)


def table_body(ids, p0, p1, p2, p3, out):
    for k, piece in enumerate((p0, p1, p2, p3)):
        out[pl.ds(4 * ((ids[0] - k) & 3), 4)] = piece[...]


def table(ids, pieces):
    return local(table_body, [((16, 64, 128), BF16)], [ids, *pieces])[0]


def halves_body(ids, p0, p1, p2, p3, low, high):
    for k, piece in enumerate((p0, p1, p2, p3)):
        at = pl.ds(4 * ((ids[0] - k) & 3), 4)
        low[at] = piece[:, :32, :]
        high[at] = piece[:, 32:, :]


def halves(ids, pieces):
    return local(halves_body, [((16, 32, 128), BF16)] * 2, [ids, *pieces])


def spread_z(pieces):
    return [pieces[0]] + [over_z(pieces[k], k) for k in (1, 2, 3)]


def edge_loop(c, meta, one):
    def band(n, _):
        row = (2 * (n >> 2) + c) * 64 + (n & 3) * 4
        one(n * 4, [(meta[row + 32 + e], meta[row + 48 + e]) for e in range(4)])
        return 0

    lax.fori_loop(0, 16, band, 0)


def proc_body(ids, meta, masks, *rest):
    tables, (own, other, ext, acc) = rest[:6], rest[6:]
    c = ids[1]
    at_own = pl.ds(pl.multiple_of(64 * c, 64), 64)
    at_other = pl.ds(pl.multiple_of(64 * (1 - c), 64), 64)
    for k in range(3):
        ext[16 * k : 16 * k + 16, at_own, :] = tables[2 * k][...]
        ext[16 * k : 16 * k + 16, at_other, :] = tables[2 * k + 1][...]
    acc[...] = jnp.zeros_like(acc)

    def one(base, edges):
        terms = [dot(masks[base + e], ext[source]) for e, (source, _) in enumerate(edges)]
        for term, (_, target) in zip(terms, edges):
            acc[target] += term

    edge_loop(c, meta, one)
    own[...] = acc[:, at_own, :]
    other[...] = acc[:, at_other, :].astype(BF16)


def proc_back_body(ids, meta, masks, mine, theirs, own, other, grads, acc):
    c = ids[1]
    at_own = pl.ds(pl.multiple_of(64 * c, 64), 64)
    at_other = pl.ds(pl.multiple_of(64 * (1 - c), 64), 64)
    grads[:, at_own, :] = mine[...]
    grads[:, at_other, :] = theirs[...]
    acc[...] = jnp.zeros_like(acc)

    def one(base, edges):
        terms = [dot(masks[base + e], grads[target]) for e, (_, target) in enumerate(edges)]
        for term, (source, _) in zip(terms, edges):
            acc[source] += term

    edge_loop(c, meta, one)
    own[...] = acc[:, at_own, :]
    other[...] = acc[:, at_other, :].astype(BF16)


def pair_sum_body(ids, own, other, *outs):
    for k in range(4):
        at = pl.ds(4 * ((ids[0] + k) & 3), 4)
        outs[k][...] = (own[at] + other[at].astype(F32)).astype(BF16)


def part_sum_body(own, other, *outs):
    for k in range(3):
        at = slice(16 * k, 16 * k + 16)
        outs[k][...] = (own[at] + other[at].astype(F32)).astype(BF16)


def three_sum_body(ids, a, b, c, *outs):
    for k in range(4):
        at = pl.ds(4 * ((ids[0] + k) & 3), 4)
        outs[k][...] = (a[at].astype(F32) + b[at].astype(F32) + c[at].astype(F32)).astype(BF16)


def fetch_body(y_first, ids, meta, t0, t1, t2, t3, *rest):
    outs, tab = rest[:8], rest[8]
    z, c, x, y = ids[0], ids[1], ids[2], ids[3]
    for k, part in enumerate((t0, t1, t2, t3)):
        tab[64 * k : 64 * k + 64] = part[...].reshape(64, 32, 128)
    for (dz, dc), out in zip(PIECES, outs):
        row = (2 * ((z + dz) & 3) + (c ^ dc)) * 64

        def take(e, _):
            slot = meta[row + e]
            kx = (x - (slot >> 6)) & 3
            ky = (y - ((slot >> 4) & 3)) & 3
            at = (kx * 4 + ky) if y_first else (ky * 4 + kx)
            out[e] = tab[at * 16 + (slot & 15)]
            return 0

        lax.fori_loop(0, 32, take, 0, unroll=4)


def fetch(y_first, ids, meta, tables):
    return local(
        functools.partial(fetch_body, y_first),
        [((32, 32, 128), BF16)] * 8,
        [ids, meta, *tables],
        smem=2,
        scratch=[pltpu.VMEM((256, 32, 128), BF16)],
    )


def grid_body(ids, source, w_send, mask, *rest):
    pieces, (out, acc, wide) = rest[:16], rest[16:]
    step = pl.program_id(0)
    z, c = ids[0], ids[1]

    @pl.when(step == 0)
    def _():
        acc[...] = jnp.zeros_like(acc)

    for k in range(4):
        for h in range(2):
            for n, (dz, dc) in enumerate(PIECES):
                at = pl.ds(pl.multiple_of(64 * (c ^ dc) + 32 * h, 32), 32)
                wide[k, at, lanes(z - dz)] = pieces[8 * h + n][k]
        at = pl.ds(pl.multiple_of(source[step * 4 + k] * 128, 128), 128)
        acc[at, :] += dot(mask[k].astype(F32).astype(BF16), wide[k])

    @pl.when(step == 7)
    def _():
        def rows(i, _):
            at = pl.ds(pl.multiple_of(i * 256, 256), 256)
            out[at, :] = dot_t(acc[at, :].astype(BF16), w_send[...]).astype(BF16)
            return 0

        lax.fori_loop(0, 12, rows, 0)


def grid_gradient(ids, source, w_send, mask, pieces):
    whole = lambda i: (0, 0)
    return pl.pallas_call(
        grid_body,
        grid=(8,),
        out_shape=jax.ShapeDtypeStruct((3072, 512), BF16),
        in_specs=[
            SMEM,
            SMEM,
            pl.BlockSpec((512, 512), whole, pipeline_mode=pl.Buffered(1)),
            pl.BlockSpec((4, 128, 128), lambda i: (i, 0, 0)),
        ]
        + [pl.BlockSpec((4, 32, 128), lambda i: (i, 0, 0))] * 16,
        out_specs=pl.BlockSpec((3072, 512), whole),
        scratch_shapes=[pltpu.VMEM((3072, 512), F32), pltpu.VMEM((4, 128, 512), BF16)],
        compiler_params=pltpu.CompilerParams(vmem_limit_bytes=32 * MIB),
    )(ids, source, w_send, mask, *pieces)


def column_exchange(pieces):
    return [pieces[0]] + [over_column(pieces[n], dz, dc) for n, (dz, dc) in enumerate(PIECES) if n]


def own_rows(array, z, c):
    cut = lax.dynamic_slice(array.reshape(4, 4, 2, 64, 512), (z, 0, c, 0, 0), (1, 4, 1, 64, 512))
    return cut.reshape(256, 512)


def per_device(
    grid_latent,
    mesh_latent,
    mesh_cotangent,
    w_send,
    w_self_enc,
    w_agg_enc,
    w_out_enc,
    w_pass,
    w_self_proc,
    w_agg_proc,
    w_out_proc,
    enc_source,
    enc_part,
    enc_block,
    enc_mask,
    proc_source,
    proc_target,
    proc_mask,
):
    g, p = lax.axis_index("grid"), lax.axis_index("mesh")
    z, c = g // 2, g % 2
    ids = jnp.stack([z, c, p // 4, p % 4]).astype(jnp.int32)
    slots = enc_part[:, 0] * 16 + enc_block
    meta = lax.all_gather(jnp.concatenate([slots, proc_source, proc_target]), "grid", axis=0, tiled=True)

    messages = send_messages(ids, enc_source, grid_latent, w_send, enc_mask)
    arrived = column_exchange(messages[:8])
    masks = lax.all_gather(
        proc_mask.astype(BF16),
        "grid",
        axis=0,
        tiled=True,
        axis_index_groups=[[2 * i + j for i in range(4)] for j in range(2)],
    )
    masks_t = jnp.swapaxes(masks, 1, 2)
    second, arrived = lax.optimization_barrier((tuple(messages[8:]), tuple(arrived)))
    arrived_2 = column_exchange(second)
    a = combine(True, ids, meta, arrived)
    a = add_rows([a[0]] + [over_y(a[k], k) for k in (1, 2, 3)])
    a = [a[0]] + [over_x(a[k], k) for k in (1, 2, 3)]
    b = combine(False, ids, meta, arrived_2)
    b = add_rows([b[0]] + [over_x(b[k], k) for k in (1, 2, 3)])
    b = [b[0]] + [over_y(b[k], k) for k in (1, 2, 3)]
    summed = spread_z(add_last(ids, a, b))

    rows = own_rows(mesh_latent, z, c)
    cotangent = own_rows(mesh_cotangent, z, c)
    pre_self = dot(rows, w_self_enc)
    g_hid_proc = lax.dot_general(
        cotangent, w_out_proc, (((1,), (1,)), ((), ())), preferred_element_type=F32
    ).astype(BF16)
    pre_enc, first, *passed = local(
        enc_mlp_body,
        [ROWS32, ROWS] + [PIECE] * 4,
        [ids, *summed, pre_self, rows, w_agg_enc, w_out_enc, w_pass],
        scratch=[WIDE],
    )

    own = table(ids, spread_z(passed))
    tables = [over_mesh(own, 1), own, over_mesh(own, -1)]
    both = []
    for one in tables:
        both += [one, over_column(one, 0, 1)]
    mine, theirs = local(
        proc_body,
        [((16, 64, 128), F32), ((16, 64, 128), BF16)],
        [ids, meta, masks_t, *both],
        smem=2,
        scratch=[pltpu.VMEM((48, 128, 128), BF16), pltpu.VMEM((16, 128, 128), F32)],
    )
    summed = local(pair_sum_body, [PIECE] * 4, [ids, mine, over_column(theirs, 0, 1)])
    pre_self_proc = dot(first, w_self_proc)
    out_rows, g_pre_proc, *g_agg = local(
        proc_mlp_body,
        [ROWS, ROWS] + [PIECE] * 4,
        [ids, *spread_z(summed), pre_self_proc, first, g_hid_proc, w_agg_proc, w_out_proc],
        scratch=[WIDE],
    )
    mesh_out = lax.all_gather(out_rows.reshape(1, 4, 64, 512), "grid", axis=0, tiled=True)
    mesh_out = jnp.swapaxes(mesh_out.reshape(4, 2, 4, 64, 512), 1, 2).reshape(2048, 512)

    g_first_part = cotangent.astype(F32) + dot_t(g_pre_proc, w_self_proc)
    own = table(ids, spread_z(g_agg))
    mine, theirs = local(
        proc_back_body,
        [((48, 64, 128), F32), ((48, 64, 128), BF16)],
        [ids, meta, masks, own, over_column(own, 0, 1)],
        smem=2,
        scratch=[pltpu.VMEM((16, 128, 128), BF16), pltpu.VMEM((48, 128, 128), F32)],
    )
    parts = local(part_sum_body, [((16, 64, 128), BF16)] * 3, [mine, over_column(theirs, 0, 1)], smem=0)
    g_pass = local(
        three_sum_body, [PIECE] * 4, [ids, over_mesh(parts[0], -1), parts[1], over_mesh(parts[2], 1)]
    )
    g_agg = local(
        enc_back_body,
        [PIECE] * 4,
        [ids, *spread_z(g_pass), g_first_part, pre_enc, w_pass, w_out_enc, w_agg_enc],
        scratch=[WIDE],
    )

    a, b = halves(ids, spread_z(g_agg))
    a = jnp.stack([a] + [over_x(a, k) for k in (1, 2, 3)])
    a = fetch(False, ids, meta, [a] + [over_y(a, k) for k in (1, 2, 3)])
    back = column_exchange(a)
    b = jnp.stack([b] + [over_y(b, k) for k in (1, 2, 3)])
    b = fetch(True, ids, meta, [b] + [over_x(b, k) for k in (1, 2, 3)])
    b, back = lax.optimization_barrier((tuple(b), tuple(back)))
    back_2 = column_exchange(b)
    grid_grad = grid_gradient(ids, enc_source, w_send, enc_mask, [*back, *back_2])
    return (mesh_out, grid_grad)


def solution(mesh):
    return jax.shard_map(
        per_device,
        mesh=mesh,
        in_specs=(
            P(("grid", "mesh"), None),
            P("mesh", None),
            P("mesh", None),
            P(),
            P(),
            P(),
            P(),
            P(),
            P(),
            P(),
            P(),
            P(("grid", "mesh")),
            P(("grid", "mesh"), None),
            P(("grid", "mesh")),
            P(("grid", "mesh"), None, None),
            P(("grid", "mesh")),
            P(("grid", "mesh")),
            P(("grid", "mesh"), None, None),
        ),
        out_specs=(P("mesh", None), P(("grid", "mesh"), None)),
        check_vma=False,
    )
```

```python
import functools

import jax
import jax.numpy as jnp
from jax import lax
from jax.experimental import pallas as pl
from jax.experimental.pallas import tpu as pltpu
from jax.sharding import PartitionSpec as P

BF16 = jnp.bfloat16
F32 = jnp.float32
MIB = 1024 * 1024
SMEM = pl.BlockSpec(memory_space=pltpu.SMEM)
VMEM = pl.BlockSpec(memory_space=pltpu.VMEM)
HBM = pl.BlockSpec(memory_space=pl.ANY)


def over_z(array, by):
    return lax.ppermute(array, "grid", [(2 * z + c, 2 * ((z + by) % 4) + c) for z in range(4) for c in range(2)])


def over_column(array, dz, dc):
    return lax.ppermute(
        array, "grid", [(2 * z + c, 2 * ((z + dz) % 4) + (c ^ dc)) for z in range(4) for c in range(2)]
    )


def over_x(array, by):
    return lax.ppermute(array, "mesh", [(4 * x + y, 4 * ((x + by) % 4) + y) for x in range(4) for y in range(4)])


def over_y(array, by):
    return lax.ppermute(array, "mesh", [(4 * x + y, 4 * x + (y + by) % 4) for x in range(4) for y in range(4)])


def over_mesh(array, by):
    return lax.ppermute(array, "mesh", [(p, (p + by) % 16) for p in range(16)])


def local(body, outs, ins, smem=1, scratch=(), limit=12):
    return pl.pallas_call(
        body,
        out_shape=[jax.ShapeDtypeStruct(shape, dtype) for shape, dtype in outs],
        in_specs=[SMEM] * smem + [VMEM] * (len(ins) - smem),
        out_specs=[VMEM] * len(outs),
        scratch_shapes=list(scratch),
        compiler_params=pltpu.CompilerParams(vmem_limit_bytes=limit * MIB),
    )(*ins)


def lanes(index):
    return pl.ds(pl.multiple_of((index & 3) * 128, 128), 128)


def dot(a, b):
    return jnp.dot(a, b, preferred_element_type=F32)


def dot_t(a, b):
    return lax.dot_general(a, b, (((1,), (1,)), ((), ())), preferred_element_type=F32)


def silu_slope(values):
    sigmoid_v = jax.nn.sigmoid(values)
    return sigmoid_v * (1.0 + values * (1.0 - sigmoid_v))


def move(source, target, sems, i):
    return pltpu.make_async_copy(source, target, sems.at[i])


def messages_body(
    source, latent, w_send, mask, other, out, other_out, x, w, m, o, sent, msg, o_b, s_x, s_w, s_m, s_o, s_out
):
    def x_in(i):
        at = pl.ds(pl.multiple_of(i * 512, 512), 512)
        return move(latent.at[at, :], x.at[at, :], s_x, i)

    def m_in(i):
        return move(mask.at[pl.ds(i * 8, 8)], m.at[pl.ds(i * 8, 8)], s_m, i)

    def out_to(i):
        return move(msg.at[:, pl.ds(i * 8, 8)], out.at[:, pl.ds(i * 8, 8)], s_out, i)

    w_in, o_in, o_to = move(w_send, w, s_w, 0), move(other, o, s_o, 0), move(o_b, other_out, s_o, 1)
    w_in.start()
    for i in range(6):
        x_in(i).start()
    for i in range(4):
        m_in(i).start()
    o_in.start()
    w_in.wait()

    def rows(i, _):
        x_in(i).wait()
        at = pl.ds(pl.multiple_of(i * 512, 512), 512)
        sent[at, :] = dot(x[at, :], w[...]).astype(BF16)
        return 0

    lax.fori_loop(0, 6, rows, 0)

    def edges(i, _):
        m_in(i).wait()
        for k in range(8):
            e = i * 8 + k
            block = sent[pl.ds(pl.multiple_of(source[e] * 128, 128), 128), :]
            message = lax.dot_general(
                m[e].astype(F32).astype(BF16), block, (((0,), (0,)), ((), ())), preferred_element_type=F32
            ).astype(BF16)
            for n in range(8):
                z, c = n // 2, n % 2
                msg[n, e] = message[64 * c : 64 * c + 64, 128 * z : 128 * z + 128]
        out_to(i).start()
        return 0

    lax.fori_loop(0, 4, edges, 0)
    o_in.wait()
    o_b[...] = o[...].astype(F32).astype(BF16)
    o_to.start()
    for i in range(4):
        out_to(i).wait()
    o_to.wait()


def send_messages(source, latent, w_send, mask, other):
    sems = lambda n: pltpu.SemaphoreType.DMA((n,))
    return pl.pallas_call(
        messages_body,
        out_shape=[
            jax.ShapeDtypeStruct((8, 32, 64, 128), BF16),
            jax.ShapeDtypeStruct((16, 128, 128), BF16),
        ],
        in_specs=[SMEM, HBM, HBM, HBM, HBM],
        out_specs=[HBM, HBM],
        scratch_shapes=[
            pltpu.VMEM((3072, 512), BF16),
            pltpu.VMEM((512, 512), BF16),
            pltpu.VMEM((32, 128, 128), jnp.int32),
            pltpu.VMEM((16, 128, 128), jnp.int32),
            pltpu.VMEM((3072, 512), BF16),
            pltpu.VMEM((8, 32, 64, 128), BF16),
            pltpu.VMEM((16, 128, 128), BF16),
            sems(6),
            sems(1),
            sems(4),
            sems(2),
            sems(4),
        ],
        compiler_params=pltpu.CompilerParams(vmem_limit_bytes=56 * MIB),
    )(source, latent, w_send, mask, other)


def combine_body(ids, meta, arrived, *rest):
    outs, acc = rest[:8], rest[8]
    x, y = ids[2], ids[3]
    acc[...] = jnp.zeros_like(acc)

    def add(n, _):
        acc[meta[(n >> 5) * 64 + (n & 31)]] += arrived[n].astype(F32)
        return 0

    lax.fori_loop(0, 256, add, 0, unroll=4)
    for kx in range(4):
        for ky in range(4):
            at = pl.ds((4 * ((x + kx) & 3) + ((y + ky) & 3)) * 16, 16)
            outs[ky][kx] = acc[at, :32, :].astype(BF16)
            outs[4 + kx][ky] = acc[at, 32:, :].astype(BF16)


def combine(ids, meta, arrived):
    outs = local(
        combine_body,
        [((4, 16, 32, 128), BF16)] * 8,
        [ids, meta, arrived.reshape(256, 64, 128)],
        smem=2,
        scratch=[pltpu.VMEM((256, 64, 128), F32)],
        limit=20,
    )
    return outs[:4], outs[4:]


def add_rows_body(*refs):
    for q in range(2):
        a, b, c, d = refs[4 * q : 4 * q + 4]
        for j in range(4):
            refs[8 + 4 * q + j][...] = (
                a[j].astype(F32) + b[j].astype(F32) + c[j].astype(F32) + d[j].astype(F32)
            ).astype(BF16)


def reduce_halves(by_y, by_x):
    by_y = [by_y[0]] + [over_y(by_y[k], k) for k in (1, 2, 3)]
    by_x = [by_x[0]] + [over_x(by_x[k], k) for k in (1, 2, 3)]
    sums = local(add_rows_body, [((16, 32, 128), BF16)] * 8, [*by_y, *by_x], smem=0)
    left, right = sums[:4], sums[4:]
    left = [left[0]] + [over_x(left[k], k) for k in (1, 2, 3)]
    right = [right[0]] + [over_y(right[k], k) for k in (1, 2, 3)]
    return [*left, *right]


def add_last_body(ids, *rest):
    terms, outs, acc = rest[:8], rest[8:12], rest[12]
    z = ids[0]
    for q in range(2):
        total = terms[4 * q][...].astype(F32)
        for more in terms[4 * q + 1 : 4 * q + 4]:
            total += more[...].astype(F32)
        acc[:, 32 * q : 32 * q + 32, :] = total.astype(BF16)
    for k in range(4):
        outs[k][...] = acc[pl.ds(4 * ((z + k) & 3), 4)]


def add_last(ids, terms):
    return local(
        add_last_body,
        [((4, 64, 128), BF16)] * 4,
        [ids, *terms],
        scratch=[pltpu.VMEM((16, 64, 128), BF16)],
    )


def to_rows(z, pieces, wide):
    for k in range(4):
        wide[:, lanes(z - k)] = pieces[k][...].reshape(256, 128)
    return wide[...]


def from_rows(z, wide, outs):
    for k in range(4):
        outs[k][...] = wide[:, lanes(z + k)].reshape(4, 64, 128)


def enc_mlp_body(ids, p0, p1, p2, p3, pre_self, rows, w_agg, w_out, w_pass, pre_ref, first_ref, *rest):
    outs, wide = rest[:4], rest[4]
    z = ids[0]
    summed = to_rows(z, (p0, p1, p2, p3), wide)
    pre = pre_self[...] + dot(summed, w_agg[...])
    pre_ref[...] = pre
    hidden = jax.nn.silu(pre).astype(BF16)
    first = (rows[...].astype(F32) + dot(hidden, w_out[...])).astype(BF16)
    first_ref[...] = first
    wide[...] = dot(first, w_pass[...]).astype(BF16)
    from_rows(z, wide, outs)


def proc_mlp_body(ids, p0, p1, p2, p3, pre_self, rows, g_hidden, w_agg, w_out, out_ref, g_pre_ref, *rest):
    outs, wide = rest[:4], rest[4]
    z = ids[0]
    summed = to_rows(z, (p0, p1, p2, p3), wide)
    pre = pre_self[...] + dot(summed, w_agg[...])
    g_pre = (g_hidden[...].astype(F32) * silu_slope(pre)).astype(BF16)
    g_pre_ref[...] = g_pre
    wide[...] = dot_t(g_pre, w_agg[...]).astype(BF16)
    from_rows(z, wide, outs)
    hidden = jax.nn.silu(pre).astype(BF16)
    out_ref[...] = (rows[...].astype(F32) + dot(hidden, w_out[...])).astype(BF16)


def enc_back_body(ids, p0, p1, p2, p3, g_part, pre, w_pass, w_out, w_agg, *rest):
    outs, wide = rest[:4], rest[4]
    z = ids[0]
    g_pass = to_rows(z, (p0, p1, p2, p3), wide)
    g_first = (g_part[...] + dot_t(g_pass, w_pass[...])).astype(BF16)
    g_hidden = dot_t(g_first, w_out[...]).astype(BF16)
    g_pre = (g_hidden.astype(F32) * silu_slope(pre[...])).astype(BF16)
    wide[...] = dot_t(g_pre, w_agg[...]).astype(BF16)
    from_rows(z, wide, outs)


ROWS = ((256, 512), BF16)
ROWS32 = ((256, 512), F32)
PIECE = ((4, 64, 128), BF16)
WIDE = pltpu.VMEM((256, 512), BF16)


def table_body(ids, p0, p1, p2, p3, out):
    for k, piece in enumerate((p0, p1, p2, p3)):
        out[pl.ds(4 * ((ids[0] - k) & 3), 4)] = piece[...]


def table(ids, pieces):
    return local(table_body, [((16, 64, 128), BF16)], [ids, *pieces])[0]


def halves_body(ids, p0, p1, p2, p3, left, right):
    for k, piece in enumerate((p0, p1, p2, p3)):
        at = pl.ds(4 * ((ids[0] - k) & 3), 4)
        left[at] = piece[:, :32, :]
        right[at] = piece[:, 32:, :]


def halves(ids, pieces):
    return local(halves_body, [((16, 32, 128), BF16)] * 2, [ids, *pieces])


def stack_body(*refs):
    for k in range(4):
        refs[8][k] = refs[k][...]
        refs[9][k] = refs[4 + k][...]


def gather_halves(left, right):
    left = [left] + [over_x(left, k) for k in (1, 2, 3)]
    right = [right] + [over_y(right, k) for k in (1, 2, 3)]
    left, right = local(stack_body, [((4, 16, 32, 128), BF16)] * 2, [*left, *right], smem=0)
    return [left] + [over_y(left, k) for k in (1, 2, 3)] + [right] + [over_x(right, k) for k in (1, 2, 3)]


def spread_z(pieces):
    return [pieces[0]] + [over_z(pieces[k], k) for k in (1, 2, 3)]


def edge_loop(c, meta, one):
    def band(n, _):
        row = (2 * (n >> 2) + c) * 64 + (n & 3) * 4
        one(n * 4, [(meta[row + 32 + e], meta[row + 48 + e]) for e in range(4)])
        return 0

    lax.fori_loop(0, 16, band, 0)


def proc_body(ids, meta, masks, *rest):
    tables, (own, other, ext, acc) = rest[:6], rest[6:]
    c = ids[1]
    at_own = pl.ds(pl.multiple_of(64 * c, 64), 64)
    at_other = pl.ds(pl.multiple_of(64 * (1 - c), 64), 64)
    for k in range(3):
        ext[16 * k : 16 * k + 16, at_own, :] = tables[2 * k][...]
        ext[16 * k : 16 * k + 16, at_other, :] = tables[2 * k + 1][...]
    acc[...] = jnp.zeros_like(acc)

    def one(base, edges):
        terms = [
            lax.dot_general(masks[base + e], ext[source], (((0,), (0,)), ((), ())), preferred_element_type=F32)
            for e, (source, _) in enumerate(edges)
        ]
        for term, (_, target) in zip(terms, edges):
            acc[target] += term

    edge_loop(c, meta, one)
    own[...] = acc[:, at_own, :]
    other[...] = acc[:, at_other, :].astype(BF16)


def proc_back_body(ids, meta, masks, mine, theirs, own, other, grads, acc):
    c = ids[1]
    at_own = pl.ds(pl.multiple_of(64 * c, 64), 64)
    at_other = pl.ds(pl.multiple_of(64 * (1 - c), 64), 64)
    grads[:, at_own, :] = mine[...]
    grads[:, at_other, :] = theirs[...]
    acc[...] = jnp.zeros_like(acc)

    def one(base, edges):
        terms = [dot(masks[base + e], grads[target]) for e, (_, target) in enumerate(edges)]
        for term, (source, _) in zip(terms, edges):
            acc[source] += term

    edge_loop(c, meta, one)
    own[...] = acc[:, at_own, :]
    other[...] = acc[:, at_other, :].astype(BF16)


def pair_sum_body(ids, own, other, *outs):
    for k in range(4):
        at = pl.ds(4 * ((ids[0] + k) & 3), 4)
        outs[k][...] = (own[at] + other[at].astype(F32)).astype(BF16)


def part_sum_body(own, other, *outs):
    for k in range(3):
        at = slice(16 * k, 16 * k + 16)
        outs[k][...] = (own[at] + other[at].astype(F32)).astype(BF16)


def three_sum_body(ids, a, b, c, *outs):
    for k in range(4):
        at = pl.ds(4 * ((ids[0] + k) & 3), 4)
        outs[k][...] = (a[at].astype(F32) + b[at].astype(F32) + c[at].astype(F32)).astype(BF16)


def fetch_body(ids, meta, *rest):
    parts, out, tab = rest[:8], rest[8], rest[9]
    x, y, owner = ids[2], ids[3], pl.program_id(0)

    @pl.when(owner == 0)
    def _():
        for kx in range(4):
            for ky in range(4):
                at = (kx * 4 + ky) * 16
                tab[at : at + 16, :32, :] = parts[ky][kx]
                tab[at : at + 16, 32:, :] = parts[4 + kx][ky]

    def take(e, _):
        slot = meta[owner * 64 + e]
        kx = (x - (slot >> 6)) & 3
        ky = (y - ((slot >> 4) & 3)) & 3
        out[0, e] = tab[(kx * 4 + ky) * 16 + (slot & 15)]
        return 0

    lax.fori_loop(0, 32, take, 0, unroll=4)


def fetch(ids, meta, parts):
    return pl.pallas_call(
        fetch_body,
        grid=(8,),
        out_shape=jax.ShapeDtypeStruct((8, 32, 64, 128), BF16),
        in_specs=[SMEM, SMEM] + [VMEM] * 8,
        out_specs=pl.BlockSpec((1, 32, 64, 128), lambda i: (i, 0, 0, 0)),
        scratch_shapes=[pltpu.VMEM((256, 64, 128), BF16)],
        compiler_params=pltpu.CompilerParams(vmem_limit_bytes=48 * MIB),
    )(ids, meta, *parts)


def grid_body(source, w_send, mask, pieces, out, w, m, p, acc, wide, o, s_w, s_m, s_p, s_out):
    def m_in(i):
        return move(mask.at[pl.ds(i * 8, 8)], m.at[pl.ds(i * 8, 8)], s_m, i)

    def p_in(i):
        return move(pieces.at[:, pl.ds(i * 8, 8)], p.at[:, pl.ds(i * 8, 8)], s_p, i)

    def out_to(i):
        at = pl.ds(pl.multiple_of(i * 512, 512), 512)
        return move(o.at[at, :], out.at[at, :], s_out, i)

    w_in = move(w_send, w, s_w, 0)
    for i in range(4):
        p_in(i).start()
        m_in(i).start()
    w_in.start()
    acc[...] = jnp.zeros_like(acc)

    def edges(i, _):
        p_in(i).wait()
        m_in(i).wait()
        for k in range(8):
            e = i * 8 + k
            for n in range(8):
                z, c = n // 2, n % 2
                wide[k, 64 * c : 64 * c + 64, 128 * z : 128 * z + 128] = p[n, e]
        for k in range(8):
            e = i * 8 + k
            at = pl.ds(pl.multiple_of(source[e] * 128, 128), 128)
            acc[at, :] += dot(m[e].astype(F32).astype(BF16), wide[k])
        return 0

    lax.fori_loop(0, 4, edges, 0)
    w_in.wait()

    def rows(i, _):
        at = pl.ds(pl.multiple_of(i * 512, 512), 512)
        o[at, :] = dot_t(acc[at, :].astype(BF16), w[...]).astype(BF16)
        out_to(i).start()
        return 0

    lax.fori_loop(0, 6, rows, 0)
    for i in range(6):
        out_to(i).wait()


def grid_gradient(source, w_send, mask, pieces):
    sems = lambda n: pltpu.SemaphoreType.DMA((n,))
    return pl.pallas_call(
        grid_body,
        out_shape=jax.ShapeDtypeStruct((3072, 512), BF16),
        in_specs=[SMEM, HBM, HBM, HBM],
        out_specs=HBM,
        scratch_shapes=[
            pltpu.VMEM((512, 512), BF16),
            pltpu.VMEM((32, 128, 128), jnp.int32),
            pltpu.VMEM((8, 32, 64, 128), BF16),
            pltpu.VMEM((3072, 512), F32),
            pltpu.VMEM((8, 128, 512), BF16),
            pltpu.VMEM((3072, 512), BF16),
            sems(1),
            sems(4),
            sems(4),
            sems(6),
        ],
        compiler_params=pltpu.CompilerParams(vmem_limit_bytes=56 * MIB),
    )(source, w_send, mask, pieces)


def column_exchange(pieces):
    return lax.all_to_all(pieces, "grid", 0, 0, tiled=True)


def own_rows(array, z, c):
    cut = lax.dynamic_slice(array.reshape(4, 4, 2, 64, 512), (z, 0, c, 0, 0), (1, 4, 1, 64, 512))
    return cut.reshape(256, 512)


def per_device(
    grid_latent,
    mesh_latent,
    mesh_cotangent,
    w_send,
    w_self_enc,
    w_agg_enc,
    w_out_enc,
    w_pass,
    w_self_proc,
    w_agg_proc,
    w_out_proc,
    enc_source,
    enc_part,
    enc_block,
    enc_mask,
    proc_source,
    proc_target,
    proc_mask,
):
    g, p = lax.axis_index("grid"), lax.axis_index("mesh")
    z, c = g // 2, g % 2
    ids = jnp.stack([z, c, p // 4, p % 4]).astype(jnp.int32)
    slots = enc_part[:, 0] * 16 + enc_block

    labels = jnp.concatenate([slots, proc_source, proc_target])

    messages, proc_mask = send_messages(enc_source, grid_latent, w_send, enc_mask, proc_mask)
    messages, labels, mesh_latent, mesh_cotangent = lax.optimization_barrier(
        (messages, labels, mesh_latent, mesh_cotangent)
    )
    arrived = column_exchange(messages)
    rows = own_rows(mesh_latent, z, c)
    cotangent = own_rows(mesh_cotangent, z, c)
    pre_self = dot(rows, w_self_enc)
    g_hid_proc = dot_t(cotangent, w_out_proc).astype(BF16)
    labels, pre_self, g_hid_proc, rows, cotangent = lax.optimization_barrier(
        (labels, pre_self, g_hid_proc, rows, cotangent)
    )
    meta = lax.all_gather(labels, "grid", axis=0, tiled=True)
    arrived, meta, proc_mask = lax.optimization_barrier((arrived, meta, proc_mask))
    masks = lax.all_gather(
        proc_mask,
        "grid",
        axis=0,
        tiled=True,
        axis_index_groups=[[2 * i + j for i in range(4)] for j in range(2)],
    )
    summed = spread_z(add_last(ids, reduce_halves(*combine(ids, meta, arrived))))
    masks, pre_self = lax.optimization_barrier((masks, pre_self))
    pre_enc, first, *passed = local(
        enc_mlp_body,
        [ROWS32, ROWS] + [PIECE] * 4,
        [ids, *summed, pre_self, rows, w_agg_enc, w_out_enc, w_pass],
        scratch=[WIDE],
    )

    own = table(ids, spread_z(passed))
    tables = [over_mesh(own, 1), own, over_mesh(own, -1)]
    both = []
    for one in tables:
        both += [one, over_column(one, 0, 1)]
    mine, theirs = local(
        proc_body,
        [((16, 64, 128), F32), ((16, 64, 128), BF16)],
        [ids, meta, masks, *both],
        smem=2,
        scratch=[pltpu.VMEM((48, 128, 128), BF16), pltpu.VMEM((16, 128, 128), F32)],
    )
    summed = local(pair_sum_body, [PIECE] * 4, [ids, mine, over_column(theirs, 0, 1)])
    pre_self_proc = dot(first, w_self_proc)
    out_rows, g_pre_proc, *g_agg = local(
        proc_mlp_body,
        [ROWS, ROWS] + [PIECE] * 4,
        [ids, *spread_z(summed), pre_self_proc, first, g_hid_proc, w_agg_proc, w_out_proc],
        scratch=[WIDE],
    )
    g_first_part = cotangent.astype(F32) + dot_t(g_pre_proc, w_self_proc)
    own = table(ids, spread_z(g_agg))
    mine, theirs = local(
        proc_back_body,
        [((48, 64, 128), F32), ((48, 64, 128), BF16)],
        [ids, meta, masks, own, over_column(own, 0, 1)],
        smem=2,
        scratch=[pltpu.VMEM((16, 128, 128), BF16), pltpu.VMEM((48, 128, 128), F32)],
    )
    parts = local(part_sum_body, [((16, 64, 128), BF16)] * 3, [mine, over_column(theirs, 0, 1)], smem=0)
    g_pass = local(
        three_sum_body, [PIECE] * 4, [ids, over_mesh(parts[0], -1), parts[1], over_mesh(parts[2], 1)]
    )
    g_agg = local(
        enc_back_body,
        [PIECE] * 4,
        [ids, *spread_z(g_pass), g_first_part, pre_enc, w_pass, w_out_enc, w_agg_enc],
        scratch=[WIDE],
    )

    left, right = halves(ids, spread_z(g_agg))
    left, out_rows = lax.optimization_barrier((left, out_rows))
    mesh_out = lax.all_gather(out_rows.reshape(1, 4, 64, 512), "grid", axis=0, tiled=True)
    mesh_out = jnp.swapaxes(mesh_out.reshape(4, 2, 4, 64, 512), 1, 2).reshape(2048, 512)
    returned = column_exchange(fetch(ids, meta, gather_halves(left, right)))
    returned, mesh_out = lax.optimization_barrier((returned, mesh_out))
    grid_grad = grid_gradient(enc_source, w_send, enc_mask, returned)
    return (mesh_out, grid_grad)


def solution(mesh):
    return jax.shard_map(
        per_device,
        mesh=mesh,
        in_specs=(
            P(("grid", "mesh"), None),
            P("mesh", None),
            P("mesh", None),
            P(),
            P(),
            P(),
            P(),
            P(),
            P(),
            P(),
            P(),
            P(("grid", "mesh")),
            P(("grid", "mesh"), None),
            P(("grid", "mesh")),
            P(("grid", "mesh"), None, None),
            P(("grid", "mesh")),
            P(("grid", "mesh")),
            P(("grid", "mesh"), None, None),
        ),
        out_specs=(P("mesh", None), P(("grid", "mesh"), None)),
        check_vma=False,
    )
```

```python
import functools

import jax
import jax.numpy as jnp
from jax import lax
from jax.experimental import pallas as pl
from jax.experimental.pallas import tpu as pltpu
from jax.sharding import PartitionSpec as P

BF16 = jnp.bfloat16
F32 = jnp.float32
MIB = 1024 * 1024
SMEM = pl.BlockSpec(memory_space=pltpu.SMEM)
VMEM = pl.BlockSpec(memory_space=pltpu.VMEM)
HBM = pl.BlockSpec(memory_space=pl.ANY)


def over_z(array, by):
    return lax.ppermute(array, "grid", [(2 * z + c, 2 * ((z + by) % 4) + c) for z in range(4) for c in range(2)])


def over_column(array, dz, dc):
    return lax.ppermute(
        array, "grid", [(2 * z + c, 2 * ((z + dz) % 4) + (c ^ dc)) for z in range(4) for c in range(2)]
    )


def over_x(array, by):
    return lax.ppermute(array, "mesh", [(4 * x + y, 4 * ((x + by) % 4) + y) for x in range(4) for y in range(4)])


def over_y(array, by):
    return lax.ppermute(array, "mesh", [(4 * x + y, 4 * x + (y + by) % 4) for x in range(4) for y in range(4)])


def over_mesh(array, by):
    return lax.ppermute(array, "mesh", [(p, (p + by) % 16) for p in range(16)])


def local(body, outs, ins, smem=1, scratch=(), limit=12):
    return pl.pallas_call(
        body,
        out_shape=[jax.ShapeDtypeStruct(shape, dtype) for shape, dtype in outs],
        in_specs=[SMEM] * smem + [VMEM] * (len(ins) - smem),
        out_specs=[VMEM] * len(outs),
        scratch_shapes=list(scratch),
        compiler_params=pltpu.CompilerParams(vmem_limit_bytes=limit * MIB),
    )(*ins)


def lanes(index):
    return pl.ds(pl.multiple_of((index & 3) * 128, 128), 128)


def dot(a, b):
    return jnp.dot(a, b, preferred_element_type=F32)


def dot_t(a, b):
    return lax.dot_general(a, b, (((1,), (1,)), ((), ())), preferred_element_type=F32)


def silu_slope(values):
    sigmoid_v = jax.nn.sigmoid(values)
    return sigmoid_v * (1.0 + values * (1.0 - sigmoid_v))


def move(source, target, sems, i):
    return pltpu.make_async_copy(source, target, sems.at[i])


def messages_body(
    source, latent, w_send, mask, other, out, other_out, x, w, m, o, sent, msg, o_b, s_x, s_w, s_m, s_o, s_out
):
    def x_in(i):
        at = pl.ds(pl.multiple_of(i * 512, 512), 512)
        return move(latent.at[at, :], x.at[at, :], s_x, i)

    def m_in(i):
        return move(mask.at[pl.ds(i * 8, 8)], m.at[pl.ds(i * 8, 8)], s_m, i)

    def out_to(i):
        return move(msg.at[:, pl.ds(i * 8, 8)], out.at[:, pl.ds(i * 8, 8)], s_out, i)

    w_in, o_in, o_to = move(w_send, w, s_w, 0), move(other, o, s_o, 0), move(o_b, other_out, s_o, 1)
    w_in.start()
    for i in range(6):
        x_in(i).start()
    for i in range(4):
        m_in(i).start()
    o_in.start()
    w_in.wait()

    def rows(i, _):
        x_in(i).wait()
        at = pl.ds(pl.multiple_of(i * 512, 512), 512)
        sent[at, :] = dot(x[at, :], w[...]).astype(BF16)
        return 0

    lax.fori_loop(0, 6, rows, 0)

    def edges(i, _):
        m_in(i).wait()
        for k in range(8):
            e = i * 8 + k
            block = sent[pl.ds(pl.multiple_of(source[e] * 128, 128), 128), :]
            message = lax.dot_general(
                m[e].astype(F32).astype(BF16), block, (((0,), (0,)), ((), ())), preferred_element_type=F32
            ).astype(BF16)
            for n in range(8):
                msg[n, e] = message[16 * n : 16 * n + 16, :]
        out_to(i).start()
        return 0

    lax.fori_loop(0, 4, edges, 0)
    o_in.wait()
    o_b[...] = o[...].astype(F32).astype(BF16)
    o_to.start()
    for i in range(4):
        out_to(i).wait()
    o_to.wait()


def send_messages(source, latent, w_send, mask, other):
    sems = lambda n: pltpu.SemaphoreType.DMA((n,))
    return pl.pallas_call(
        messages_body,
        out_shape=[
            jax.ShapeDtypeStruct((8, 32, 16, 512), BF16),
            jax.ShapeDtypeStruct((16, 128, 128), BF16),
        ],
        in_specs=[SMEM, HBM, HBM, HBM, HBM],
        out_specs=[HBM, HBM],
        scratch_shapes=[
            pltpu.VMEM((3072, 512), BF16),
            pltpu.VMEM((512, 512), BF16),
            pltpu.VMEM((32, 128, 128), jnp.int32),
            pltpu.VMEM((16, 128, 128), jnp.int32),
            pltpu.VMEM((3072, 512), BF16),
            pltpu.VMEM((8, 32, 16, 512), BF16),
            pltpu.VMEM((16, 128, 128), BF16),
            sems(6),
            sems(1),
            sems(4),
            sems(2),
            sems(4),
        ],
        compiler_params=pltpu.CompilerParams(vmem_limit_bytes=56 * MIB),
    )(source, latent, w_send, mask, other)


def combine_body(ids, meta, arrived, *rest):
    outs, acc = rest[:8], rest[8]
    x, y = ids[2], ids[3]
    acc[...] = jnp.zeros_like(acc)

    def add(n, _):
        acc[meta[(n >> 5) * 64 + (n & 31)]] += arrived[n].astype(F32)
        return 0

    lax.fori_loop(0, 256, add, 0, unroll=4)
    for kx in range(4):
        for ky in range(4):
            at = pl.ds((4 * ((x + kx) & 3) + ((y + ky) & 3)) * 16, 16)
            outs[ky][kx] = acc[at, :, :256].astype(BF16)
            outs[4 + kx][ky] = acc[at, :, 256:].astype(BF16)


def combine(ids, meta, arrived):
    outs = local(
        combine_body,
        [((4, 16, 16, 256), BF16)] * 8,
        [ids, meta, arrived.reshape(256, 16, 512)],
        smem=2,
        scratch=[pltpu.VMEM((256, 16, 512), F32)],
        limit=20,
    )
    return outs[:4], outs[4:]


def add_rows_body(*refs):
    for q in range(2):
        a, b, c, d = refs[4 * q : 4 * q + 4]
        for j in range(4):
            refs[8 + 4 * q + j][...] = (
                a[j].astype(F32) + b[j].astype(F32) + c[j].astype(F32) + d[j].astype(F32)
            ).astype(BF16)


def reduce_halves(by_y, by_x):
    by_y = [by_y[0]] + [over_y(by_y[k], k) for k in (1, 2, 3)]
    by_x = [by_x[0]] + [over_x(by_x[k], k) for k in (1, 2, 3)]
    sums = local(add_rows_body, [((16, 16, 256), BF16)] * 8, [*by_y, *by_x], smem=0)
    left, right = sums[:4], sums[4:]
    left = [left[0]] + [over_x(left[k], k) for k in (1, 2, 3)]
    right = [right[0]] + [over_y(right[k], k) for k in (1, 2, 3)]
    return [*left, *right]


def to_rows(z, pieces, wide):
    for k in range(4):
        wide[:, lanes(z - k)] = pieces[k][...].reshape(256, 128)
    return wide[...]


def from_rows(z, wide, outs):
    for k in range(4):
        outs[k][...] = wide[:, lanes(z + k)].reshape(16, 16, 128)


def enc_mlp_body(ids, *rest):
    terms, (pre_self, rows, w_agg, w_out, w_pass, pre_ref, first_ref) = rest[:8], rest[8:15]
    outs, wide = rest[15:19], rest[19]
    z = ids[0]
    pre = pre_self[...]
    for q in range(2):
        total = terms[4 * q][...].astype(F32)
        for more in terms[4 * q + 1 : 4 * q + 4]:
            total += more[...].astype(F32)
        pre += dot(total.astype(BF16).reshape(256, 256), w_agg[256 * q : 256 * q + 256, :])
    pre_ref[...] = pre
    hidden = jax.nn.silu(pre).astype(BF16)
    first = (rows[...].astype(F32) + dot(hidden, w_out[...])).astype(BF16)
    first_ref[...] = first
    wide[...] = dot(first, w_pass[...]).astype(BF16)
    from_rows(z, wide, outs)


def proc_mlp_body(ids, p0, p1, p2, p3, pre_self, rows, g_hidden, w_agg, w_out, out_ref, g_pre_ref, *rest):
    outs, wide = rest[:4], rest[4]
    z = ids[0]
    summed = to_rows(z, (p0, p1, p2, p3), wide)
    pre = pre_self[...] + dot(summed, w_agg[...])
    g_pre = (g_hidden[...].astype(F32) * silu_slope(pre)).astype(BF16)
    g_pre_ref[...] = g_pre
    wide[...] = dot_t(g_pre, w_agg[...]).astype(BF16)
    from_rows(z, wide, outs)
    hidden = jax.nn.silu(pre).astype(BF16)
    out_ref[...] = (rows[...].astype(F32) + dot(hidden, w_out[...])).astype(BF16)


def enc_back_body(ids, p0, p1, p2, p3, g_part, pre, w_pass, w_out, w_agg, left, right, wide):
    z = ids[0]
    g_pass = to_rows(z, (p0, p1, p2, p3), wide)
    g_first = (g_part[...] + dot_t(g_pass, w_pass[...])).astype(BF16)
    g_hidden = dot_t(g_first, w_out[...]).astype(BF16)
    g_pre = (g_hidden.astype(F32) * silu_slope(pre[...])).astype(BF16)
    g_agg = dot_t(g_pre, w_agg[...]).astype(BF16)
    left[...] = g_agg[:, :256].reshape(16, 16, 256)
    right[...] = g_agg[:, 256:].reshape(16, 16, 256)


ROWS = ((256, 512), BF16)
ROWS32 = ((256, 512), F32)
PIECE = ((16, 16, 128), BF16)
WIDE = pltpu.VMEM((256, 512), BF16)


def band(z):
    return pl.ds(pl.multiple_of((z & 3) * 16, 16), 16)


def table_body(ids, p0, p1, p2, p3, out):
    for k, piece in enumerate((p0, p1, p2, p3)):
        out[:, band(ids[0] - k), :] = piece[...]


def table(ids, pieces):
    return local(table_body, [((16, 64, 128), BF16)], [ids, *pieces])[0]


def stack_body(*refs):
    for k in range(4):
        refs[8][k] = refs[k][...]
        refs[9][k] = refs[4 + k][...]


def gather_halves(left, right):
    left = [left] + [over_x(left, k) for k in (1, 2, 3)]
    right = [right] + [over_y(right, k) for k in (1, 2, 3)]
    left, right = local(stack_body, [((4, 16, 16, 256), BF16)] * 2, [*left, *right], smem=0)
    return [left] + [over_y(left, k) for k in (1, 2, 3)] + [right] + [over_x(right, k) for k in (1, 2, 3)]


def spread_z(pieces):
    return [pieces[0]] + [over_z(pieces[k], k) for k in (1, 2, 3)]


def edge_loop(c, meta, one):
    def four(n, _):
        row = (2 * (n >> 2) + c) * 64 + (n & 3) * 4
        one(n * 4, [(meta[row + 32 + e], meta[row + 48 + e]) for e in range(4)])
        return 0

    lax.fori_loop(0, 16, four, 0)


def core_rows(z, c):
    return pl.ds(pl.multiple_of(32 * z + 16 * c, 16), 16)


def join_rows(c, mine, theirs, whole, first):
    blocks = mine.shape[0]
    for z in range(4):
        at = slice(16 * z, 16 * z + 16)
        whole[first : first + blocks, core_rows(z, c), :] = mine[:, at, :]
        whole[first : first + blocks, core_rows(z, 1 - c), :] = theirs[:, at, :]


def part_rows(c, whole, own, other):
    for z in range(4):
        at = slice(16 * z, 16 * z + 16)
        own[:, at, :] = whole[:, core_rows(z, c), :]
        other[:, at, :] = whole[:, core_rows(z, 1 - c), :].astype(BF16)


def proc_body(ids, meta, masks, *rest):
    tables, (own, other, ext, acc) = rest[:6], rest[6:]
    c = ids[1]
    for k in range(3):
        join_rows(c, tables[2 * k], tables[2 * k + 1], ext, 16 * k)
    acc[...] = jnp.zeros_like(acc)

    def one(base, edges):
        terms = [
            lax.dot_general(masks[base + e], ext[source], (((0,), (0,)), ((), ())), preferred_element_type=F32)
            for e, (source, _) in enumerate(edges)
        ]
        for term, (_, target) in zip(terms, edges):
            acc[target] += term

    edge_loop(c, meta, one)
    part_rows(c, acc, own, other)


def proc_back_body(ids, meta, masks, mine, theirs, own, other, grads, acc):
    c = ids[1]
    join_rows(c, mine, theirs, grads, 0)
    acc[...] = jnp.zeros_like(acc)

    def one(base, edges):
        terms = [dot(masks[base + e], grads[target]) for e, (_, target) in enumerate(edges)]
        for term, (source, _) in zip(terms, edges):
            acc[source] += term

    edge_loop(c, meta, one)
    part_rows(c, acc, own, other)


def pair_sum_body(ids, own, other, *outs):
    for k in range(4):
        at = band(ids[0] + k)
        outs[k][...] = (own[:, at, :] + other[:, at, :].astype(F32)).astype(BF16)


def part_sum_body(own, other, *outs):
    for k in range(3):
        at = slice(16 * k, 16 * k + 16)
        outs[k][...] = (own[at] + other[at].astype(F32)).astype(BF16)


def three_sum_body(ids, a, b, c, *outs):
    for k in range(4):
        at = band(ids[0] + k)
        total = a[:, at, :].astype(F32) + b[:, at, :].astype(F32) + c[:, at, :].astype(F32)
        outs[k][...] = total.astype(BF16)


def fetch_body(ids, meta, *rest):
    parts, (out, tab, picked, sems) = rest[:8], rest[8:]
    x, y = ids[2], ids[3]
    for kx in range(4):
        for ky in range(4):
            at = (kx * 4 + ky) * 16
            tab[at : at + 16, :, :256] = parts[ky][kx]
            tab[at : at + 16, :, 256:] = parts[4 + kx][ky]

    def out_to(i):
        return move(picked.at[i], out.at[i], sems, i)

    def owner(i, _):
        for e in range(32):
            slot = meta[i * 64 + e]
            kx = (x - (slot >> 6)) & 3
            ky = (y - ((slot >> 4) & 3)) & 3
            picked[i, e] = tab[(kx * 4 + ky) * 16 + (slot & 15)]
        out_to(i).start()
        return 0

    lax.fori_loop(0, 8, owner, 0)
    for i in range(8):
        out_to(i).wait()


def fetch(ids, meta, parts):
    return pl.pallas_call(
        fetch_body,
        out_shape=jax.ShapeDtypeStruct((8, 32, 16, 512), BF16),
        in_specs=[SMEM, SMEM] + [VMEM] * 8,
        out_specs=HBM,
        scratch_shapes=[
            pltpu.VMEM((256, 16, 512), BF16),
            pltpu.VMEM((8, 32, 16, 512), BF16),
            pltpu.SemaphoreType.DMA((8,)),
        ],
        compiler_params=pltpu.CompilerParams(vmem_limit_bytes=48 * MIB),
    )(ids, meta, *parts)


def grid_body(source, w_send, mask, pieces, out, w, m, p, acc, wide, o, s_w, s_m, s_p, s_out):
    def m_in(i):
        return move(mask.at[pl.ds(i * 8, 8)], m.at[pl.ds(i * 8, 8)], s_m, i)

    def p_in(i):
        return move(pieces.at[:, pl.ds(i * 8, 8)], p.at[:, pl.ds(i * 8, 8)], s_p, i)

    def out_to(i):
        at = pl.ds(pl.multiple_of(i * 512, 512), 512)
        return move(o.at[at, :], out.at[at, :], s_out, i)

    w_in = move(w_send, w, s_w, 0)
    for i in range(4):
        p_in(i).start()
        m_in(i).start()
    w_in.start()
    acc[...] = jnp.zeros_like(acc)

    def edges(i, _):
        p_in(i).wait()
        m_in(i).wait()
        for k in range(8):
            e = i * 8 + k
            for n in range(8):
                wide[k, 16 * n : 16 * n + 16, :] = p[n, e]
        for k in range(8):
            e = i * 8 + k
            at = pl.ds(pl.multiple_of(source[e] * 128, 128), 128)
            acc[at, :] += dot(m[e].astype(F32).astype(BF16), wide[k])
        return 0

    lax.fori_loop(0, 4, edges, 0)
    w_in.wait()

    def rows(i, _):
        at = pl.ds(pl.multiple_of(i * 512, 512), 512)
        o[at, :] = dot_t(acc[at, :].astype(BF16), w[...]).astype(BF16)
        out_to(i).start()
        return 0

    lax.fori_loop(0, 6, rows, 0)
    for i in range(6):
        out_to(i).wait()


def grid_gradient(source, w_send, mask, pieces):
    sems = lambda n: pltpu.SemaphoreType.DMA((n,))
    return pl.pallas_call(
        grid_body,
        out_shape=jax.ShapeDtypeStruct((3072, 512), BF16),
        in_specs=[SMEM, HBM, HBM, HBM],
        out_specs=HBM,
        scratch_shapes=[
            pltpu.VMEM((512, 512), BF16),
            pltpu.VMEM((32, 128, 128), jnp.int32),
            pltpu.VMEM((8, 32, 16, 512), BF16),
            pltpu.VMEM((3072, 512), F32),
            pltpu.VMEM((8, 128, 512), BF16),
            pltpu.VMEM((3072, 512), BF16),
            sems(1),
            sems(4),
            sems(4),
            sems(6),
        ],
        compiler_params=pltpu.CompilerParams(vmem_limit_bytes=56 * MIB),
    )(source, w_send, mask, pieces)


def column_exchange(pieces):
    return lax.all_to_all(pieces, "grid", 0, 0, tiled=True)


def own_rows(array, g):
    return lax.dynamic_index_in_dim(array.reshape(16, 8, 16, 512), g, 1, False).reshape(256, 512)


def per_device(
    grid_latent,
    mesh_latent,
    mesh_cotangent,
    w_send,
    w_self_enc,
    w_agg_enc,
    w_out_enc,
    w_pass,
    w_self_proc,
    w_agg_proc,
    w_out_proc,
    enc_source,
    enc_part,
    enc_block,
    enc_mask,
    proc_source,
    proc_target,
    proc_mask,
):
    g, p = lax.axis_index("grid"), lax.axis_index("mesh")
    z, c = g // 2, g % 2
    ids = jnp.stack([z, c, p // 4, p % 4]).astype(jnp.int32)
    slots = enc_part[:, 0] * 16 + enc_block

    labels = jnp.concatenate([slots, proc_source, proc_target])

    messages, proc_mask = send_messages(enc_source, grid_latent, w_send, enc_mask, proc_mask)
    messages, labels, mesh_latent, mesh_cotangent = lax.optimization_barrier(
        (messages, labels, mesh_latent, mesh_cotangent)
    )
    arrived = column_exchange(messages)
    rows = own_rows(mesh_latent, g)
    cotangent = own_rows(mesh_cotangent, g)
    pre_self = dot(rows, w_self_enc)
    g_hid_proc = dot_t(cotangent, w_out_proc).astype(BF16)
    labels, pre_self, g_hid_proc, rows, cotangent = lax.optimization_barrier(
        (labels, pre_self, g_hid_proc, rows, cotangent)
    )
    meta = lax.all_gather(labels, "grid", axis=0, tiled=True)
    arrived, meta, proc_mask = lax.optimization_barrier((arrived, meta, proc_mask))
    masks = lax.all_gather(
        proc_mask,
        "grid",
        axis=0,
        tiled=True,
        axis_index_groups=[[2 * i + j for i in range(4)] for j in range(2)],
    )
    summed = reduce_halves(*combine(ids, meta, arrived))
    pre_enc, first, *passed = local(
        enc_mlp_body,
        [ROWS32, ROWS] + [PIECE] * 4,
        [ids, *summed, pre_self, rows, w_agg_enc, w_out_enc, w_pass],
        scratch=[WIDE],
    )

    masks, kept = lax.optimization_barrier((masks, passed[0]))
    own = table(ids, spread_z([kept, *passed[1:]]))
    tables = [over_mesh(own, 1), own, over_mesh(own, -1)]
    both = []
    for one in tables:
        both += [one, over_column(one, 0, 1)]
    mine, theirs = local(
        proc_body,
        [((16, 64, 128), F32), ((16, 64, 128), BF16)],
        [ids, meta, masks, *both],
        smem=2,
        scratch=[pltpu.VMEM((48, 128, 128), BF16), pltpu.VMEM((16, 128, 128), F32)],
    )
    summed = local(pair_sum_body, [PIECE] * 4, [ids, mine, over_column(theirs, 0, 1)])
    pre_self_proc = dot(first, w_self_proc)
    out_rows, g_pre_proc, *g_agg = local(
        proc_mlp_body,
        [ROWS, ROWS] + [PIECE] * 4,
        [ids, *spread_z(summed), pre_self_proc, first, g_hid_proc, w_agg_proc, w_out_proc],
        scratch=[WIDE],
    )
    g_first_part = cotangent.astype(F32) + dot_t(g_pre_proc, w_self_proc)
    own = table(ids, spread_z(g_agg))
    mine, theirs = local(
        proc_back_body,
        [((48, 64, 128), F32), ((48, 64, 128), BF16)],
        [ids, meta, masks, own, over_column(own, 0, 1)],
        smem=2,
        scratch=[pltpu.VMEM((16, 128, 128), BF16), pltpu.VMEM((48, 128, 128), F32)],
    )
    parts = local(part_sum_body, [((16, 64, 128), BF16)] * 3, [mine, over_column(theirs, 0, 1)], smem=0)
    g_pass = local(
        three_sum_body, [PIECE] * 4, [ids, over_mesh(parts[0], -1), parts[1], over_mesh(parts[2], 1)]
    )
    left, right = local(
        enc_back_body,
        [((16, 16, 256), BF16)] * 2,
        [ids, *spread_z(g_pass), g_first_part, pre_enc, w_pass, w_out_enc, w_agg_enc],
        scratch=[WIDE],
    )

    left, out_rows = lax.optimization_barrier((left, out_rows))
    mesh_out = lax.all_gather(out_rows.reshape(1, 16, 16, 512), "grid", axis=0, tiled=True)
    mesh_out = jnp.swapaxes(mesh_out, 0, 1).reshape(2048, 512)
    returned = column_exchange(fetch(ids, meta, gather_halves(left, right)))
    returned, mesh_out = lax.optimization_barrier((returned, mesh_out))
    grid_grad = grid_gradient(enc_source, w_send, enc_mask, returned)
    return (mesh_out, grid_grad)


def solution(mesh):
    return jax.shard_map(
        per_device,
        mesh=mesh,
        in_specs=(
            P(("grid", "mesh"), None),
            P("mesh", None),
            P("mesh", None),
            P(),
            P(),
            P(),
            P(),
            P(),
            P(),
            P(),
            P(),
            P(("grid", "mesh")),
            P(("grid", "mesh"), None),
            P(("grid", "mesh")),
            P(("grid", "mesh"), None, None),
            P(("grid", "mesh")),
            P(("grid", "mesh")),
            P(("grid", "mesh"), None, None),
        ),
        out_specs=(P("mesh", None), P(("grid", "mesh"), None)),
        check_vma=False,
    )
```

```python
import functools

import jax
import jax.numpy as jnp
from jax import lax
from jax.experimental import pallas as pl
from jax.experimental.pallas import tpu as pltpu
from jax.sharding import PartitionSpec as P

BF16 = jnp.bfloat16
F32 = jnp.float32
MIB = 1024 * 1024
SMEM = pl.BlockSpec(memory_space=pltpu.SMEM)
VMEM = pl.BlockSpec(memory_space=pltpu.VMEM)
HBM = pl.BlockSpec(memory_space=pltpu.HBM)


def over_z(array, by):
    return lax.ppermute(array, "grid", [(2 * z + c, 2 * ((z + by) % 4) + c) for z in range(4) for c in range(2)])


def over_column(array, dz, dc):
    return lax.ppermute(
        array, "grid", [(2 * z + c, 2 * ((z + dz) % 4) + (c ^ dc)) for z in range(4) for c in range(2)]
    )


def over_x(array, by):
    return lax.ppermute(array, "mesh", [(4 * x + y, 4 * ((x + by) % 4) + y) for x in range(4) for y in range(4)])


def over_y(array, by):
    return lax.ppermute(array, "mesh", [(4 * x + y, 4 * x + (y + by) % 4) for x in range(4) for y in range(4)])


def over_mesh(array, by):
    return lax.ppermute(array, "mesh", [(p, (p + by) % 16) for p in range(16)])


def local(body, outs, ins, smem=1, scratch=(), limit=12):
    return pl.pallas_call(
        body,
        out_shape=[jax.ShapeDtypeStruct(shape, dtype) for shape, dtype in outs],
        in_specs=[SMEM] * smem + [VMEM] * (len(ins) - smem),
        out_specs=[VMEM] * len(outs),
        scratch_shapes=list(scratch),
        compiler_params=pltpu.CompilerParams(vmem_limit_bytes=limit * MIB),
    )(*ins)


def lanes(index):
    return pl.ds(pl.multiple_of((index & 3) * 128, 128), 128)


def dot(a, b):
    return jnp.dot(a, b, preferred_element_type=F32)


def dot_t(a, b):
    return lax.dot_general(a, b, (((1,), (1,)), ((), ())), preferred_element_type=F32)


def silu_slope(values):
    sigmoid_v = jax.nn.sigmoid(values)
    return sigmoid_v * (1.0 + values * (1.0 - sigmoid_v))


def move(source, target, sems, i):
    return pltpu.make_async_copy(source, target, sems.at[i])


def messages_body(
    source, latent, w_send, mask, other, out, other_out, x, w, m, o, sent, msg, o_b, s_x, s_w, s_m, s_o, s_out
):
    def x_in(i):
        at = pl.ds(pl.multiple_of(i * 512, 512), 512)
        return move(latent.at[at, :], x.at[at, :], s_x, i)

    def m_in(i):
        return move(mask.at[pl.ds(i * 8, 8)], m.at[pl.ds(i * 8, 8)], s_m, i)

    def out_to(i):
        return move(msg.at[:, pl.ds(i * 8, 8)], out.at[:, pl.ds(i * 8, 8)], s_out, i)

    w_in, o_in, o_to = move(w_send, w, s_w, 0), move(other, o, s_o, 0), move(o_b, other_out, s_o, 1)
    w_in.start()
    for i in range(6):
        x_in(i).start()
    for i in range(4):
        m_in(i).start()
    o_in.start()
    w_in.wait()

    def rows(i, _):
        x_in(i).wait()
        at = pl.ds(pl.multiple_of(i * 512, 512), 512)
        sent[at, :] = dot(x[at, :], w[...]).astype(BF16)
        return 0

    lax.fori_loop(0, 6, rows, 0)

    def edges(i, _):
        m_in(i).wait()
        for k in range(8):
            e = i * 8 + k
            block = sent[pl.ds(pl.multiple_of(source[e] * 128, 128), 128), :]
            message = lax.dot_general(
                m[e].astype(F32).astype(BF16), block, (((0,), (0,)), ((), ())), preferred_element_type=F32
            ).astype(BF16)
            for n in range(8):
                msg[n, e] = message[16 * n : 16 * n + 16, :]
        out_to(i).start()
        return 0

    lax.fori_loop(0, 4, edges, 0)
    o_in.wait()
    o_b[...] = o[...].astype(F32).astype(BF16)
    o_to.start()
    for i in range(4):
        out_to(i).wait()
    o_to.wait()


def send_messages(source, latent, w_send, mask, other):
    sems = lambda n: pltpu.SemaphoreType.DMA((n,))
    return pl.pallas_call(
        messages_body,
        out_shape=[
            jax.ShapeDtypeStruct((8, 32, 16, 512), BF16),
            jax.ShapeDtypeStruct((16, 128, 128), BF16),
        ],
        in_specs=[SMEM, HBM, HBM, HBM, HBM],
        out_specs=[HBM, HBM],
        scratch_shapes=[
            pltpu.VMEM((3072, 512), BF16),
            pltpu.VMEM((512, 512), BF16),
            pltpu.VMEM((32, 128, 128), jnp.int32),
            pltpu.VMEM((16, 128, 128), jnp.int32),
            pltpu.VMEM((3072, 512), BF16),
            pltpu.VMEM((8, 32, 16, 512), BF16),
            pltpu.VMEM((16, 128, 128), BF16),
            sems(6),
            sems(1),
            sems(4),
            sems(2),
            sems(4),
        ],
        compiler_params=pltpu.CompilerParams(vmem_limit_bytes=56 * MIB),
    )(source, latent, w_send, mask, other)


def combine_body(ids, meta, arrived, *rest):
    outs, acc = rest[:10], rest[10]
    x, y = ids[2], ids[3]
    acc[...] = jnp.zeros_like(acc)

    def add(n, _):
        acc[meta[(n >> 5) * 64 + (n & 31)]] += arrived[n].astype(F32)
        return 0

    lax.fori_loop(0, 256, add, 0, unroll=4)
    for kx in range(4):
        for ky in range(4):
            at = pl.ds((4 * ((x + kx) & 3) + ((y + ky) & 3)) * 16, 16)
            place(outs[:5], ky, kx, acc[at, :, :256].astype(BF16))
            place(outs[5:], kx, ky, acc[at, :, 256:].astype(BF16))


def place(refs, step, other, value):
    if step == 2:
        refs[2 + other // 2][other % 2] = value
    else:
        refs[{0: 0, 1: 1, 3: 4}[step]][other] = value


PARTS = [((4, 16, 16, 256), BF16)] * 2 + [((2, 16, 16, 256), BF16)] * 2 + [((4, 16, 16, 256), BF16)]
SMALL = [((16, 16, 256), BF16)] * 2 + [((8, 16, 256), BF16)] * 2 + [((16, 16, 256), BF16)]


def combine(ids, meta, arrived):
    outs = local(
        combine_body,
        PARTS * 2,
        [ids, meta, arrived.reshape(256, 16, 512)],
        smem=2,
        scratch=[pltpu.VMEM((256, 16, 512), F32)],
        limit=20,
    )
    return outs[:5], outs[5:]


def relay_body(*refs):
    for q in range(2):
        on, back, from_back, from_on = refs[4 * q : 4 * q + 4]
        new_on, new_back = refs[8 + 2 * q : 10 + 2 * q]
        half = on.shape[0] // 2
        new_on[:half] = (on[:half].astype(F32) + from_back[...].astype(F32)).astype(BF16)
        new_on[half:] = on[half:]
        new_back[:half] = back[:half]
        new_back[half:] = (back[half:].astype(F32) + from_on[...].astype(F32)).astype(BF16)


def relay(first, first_over, second, second_over):
    ins = []
    for parts, over in ((first, first_over), (second, second_over)):
        ins += [parts[1], parts[4], over(parts[2], 1), over(parts[3], 3)]
    kind = (ins[0].shape, BF16)
    on_1, back_1, on_2, back_2 = local(relay_body, [kind] * 4, ins, smem=0)
    return (
        [first[0], first_over(on_1, 1), first_over(back_1, 3)],
        [second[0], second_over(on_2, 1), second_over(back_2, 3)],
    )


def add_rows_body(*refs):
    for q in range(2):
        a, b, c = refs[3 * q : 3 * q + 3]
        outs = refs[6 + 5 * q : 11 + 5 * q]
        for j in range(4):
            total = (a[j].astype(F32) + b[j].astype(F32) + c[j].astype(F32)).astype(BF16)
            if j == 2:
                outs[2][...] = total[:8]
                outs[3][...] = total[8:]
            else:
                outs[{0: 0, 1: 1, 3: 4}[j]][...] = total


def reduce_halves(by_y, by_x):
    by_y, by_x = relay(by_y, over_y, by_x, over_x)
    sums = local(add_rows_body, SMALL * 2, [*by_y, *by_x], smem=0)
    left, right = relay(sums[:5], over_x, sums[5:], over_y)
    return [*left, *right]


def to_rows(z, pieces, wide):
    for k in range(4):
        wide[:, lanes(z - k)] = pieces[k][...].reshape(256, 128)
    return wide[...]


def from_rows(z, wide, outs):
    for k in range(4):
        outs[k][...] = wide[:, lanes(z + k)].reshape(16, 16, 128)


def enc_mlp_body(ids, *rest):
    terms, (pre_self, rows, w_agg, w_out, w_pass, pre_ref, first_ref) = rest[:6], rest[6:13]
    outs, wide = rest[13:17], rest[17]
    z = ids[0]
    pre = pre_self[...]
    for q in range(2):
        a, b, c = terms[3 * q : 3 * q + 3]
        total = a[...].astype(F32) + b[...].astype(F32) + c[...].astype(F32)
        pre += dot(total.astype(BF16).reshape(256, 256), w_agg[256 * q : 256 * q + 256, :])
    pre_ref[...] = pre
    hidden = jax.nn.silu(pre).astype(BF16)
    first = (rows[...].astype(F32) + dot(hidden, w_out[...])).astype(BF16)
    first_ref[...] = first
    wide[...] = dot(first, w_pass[...]).astype(BF16)
    from_rows(z, wide, outs)


def proc_mlp_body(ids, p0, p1, p2, p3, pre_self, rows, g_hidden, w_agg, w_out, out_ref, g_pre_ref, *rest):
    outs, wide = rest[:4], rest[4]
    z = ids[0]
    summed = to_rows(z, (p0, p1, p2, p3), wide)
    pre = pre_self[...] + dot(summed, w_agg[...])
    g_pre = (g_hidden[...].astype(F32) * silu_slope(pre)).astype(BF16)
    g_pre_ref[...] = g_pre
    wide[...] = dot_t(g_pre, w_agg[...]).astype(BF16)
    from_rows(z, wide, outs)
    hidden = jax.nn.silu(pre).astype(BF16)
    out_ref[...] = (rows[...].astype(F32) + dot(hidden, w_out[...])).astype(BF16)


def enc_back_body(ids, p0, p1, p2, p3, g_part, pre, w_pass, w_out, w_agg, left, right, wide):
    z = ids[0]
    g_pass = to_rows(z, (p0, p1, p2, p3), wide)
    g_first = (g_part[...] + dot_t(g_pass, w_pass[...])).astype(BF16)
    g_hidden = dot_t(g_first, w_out[...]).astype(BF16)
    g_pre = (g_hidden.astype(F32) * silu_slope(pre[...])).astype(BF16)
    g_agg = dot_t(g_pre, w_agg[...]).astype(BF16)
    left[...] = g_agg[:, :256].reshape(16, 16, 256)
    right[...] = g_agg[:, 256:].reshape(16, 16, 256)


ROWS = ((256, 512), BF16)
ROWS32 = ((256, 512), F32)
PIECE = ((16, 16, 128), BF16)
WIDE = pltpu.VMEM((256, 512), BF16)


def band(z):
    return pl.ds(pl.multiple_of((z & 3) * 16, 16), 16)


def table_body(ids, p0, p1, p2, p3, out):
    for k, piece in enumerate((p0, p1, p2, p3)):
        out[:, band(ids[0] - k), :] = piece[...]


def table(ids, pieces):
    return local(table_body, [((16, 64, 128), BF16)], [ids, *pieces])[0]


def stack_body(*refs):
    for k in range(4):
        refs[8][k] = refs[k][...]
        refs[9][k] = refs[4 + k][...]


def gather_halves(left, right):
    left = [left] + [over_x(left, k) for k in (1, 2, 3)]
    right = [right] + [over_y(right, k) for k in (1, 2, 3)]
    left, right = local(stack_body, [((4, 16, 16, 256), BF16)] * 2, [*left, *right], smem=0)
    return [left] + [over_y(left, k) for k in (1, 2, 3)] + [right] + [over_x(right, k) for k in (1, 2, 3)]


def spread_z(pieces):
    return [pieces[0]] + [over_z(pieces[k], k) for k in (1, 2, 3)]


def edge_loop(z, c, meta, one):
    for k in range(4):
        row = (2 * ((z - k) & 3) + c) * 64

        def four(n, _):
            at = row + n * 4
            one(k, n * 4, [(meta[at + 32 + e], meta[at + 48 + e]) for e in range(4)])
            return 0

        lax.fori_loop(0, 4, four, 0)


def core_rows(z, c):
    return pl.ds(pl.multiple_of(32 * z + 16 * c, 16), 16)


def join_rows(c, mine, theirs, whole, first):
    blocks = mine.shape[0]
    for z in range(4):
        at = slice(16 * z, 16 * z + 16)
        whole[first : first + blocks, core_rows(z, c), :] = mine[:, at, :]
        whole[first : first + blocks, core_rows(z, 1 - c), :] = theirs[:, at, :]


def part_rows(c, whole, own, other):
    for z in range(4):
        at = slice(16 * z, 16 * z + 16)
        own[:, at, :] = whole[:, core_rows(z, c), :]
        other[:, at, :] = whole[:, core_rows(z, 1 - c), :].astype(BF16)


def proc_body(ids, meta, *rest):
    masks, tables, (own, other, ext, acc) = rest[:4], rest[4:10], rest[10:]
    z, c = ids[0], ids[1]
    for k in range(3):
        join_rows(c, tables[2 * k], tables[2 * k + 1], ext, 16 * k)
    acc[...] = jnp.zeros_like(acc)

    def one(k, base, edges):
        terms = [
            lax.dot_general(masks[k][base + e], ext[source], (((0,), (0,)), ((), ())), preferred_element_type=F32)
            for e, (source, _) in enumerate(edges)
        ]
        for term, (_, target) in zip(terms, edges):
            acc[target] += term

    edge_loop(z, c, meta, one)
    part_rows(c, acc, own, other)


def proc_back_body(ids, meta, *rest):
    masks, (mine, theirs, own, other, grads, acc) = rest[:4], rest[4:]
    z, c = ids[0], ids[1]
    join_rows(c, mine, theirs, grads, 0)
    acc[...] = jnp.zeros_like(acc)

    def one(k, base, edges):
        terms = [dot(masks[k][base + e], grads[target]) for e, (_, target) in enumerate(edges)]
        for term, (source, _) in zip(terms, edges):
            acc[source] += term

    edge_loop(z, c, meta, one)
    part_rows(c, acc, own, other)


def pack_body(ids, p0, p1, p2, p3, out):
    for k, piece in enumerate((p0, p1, p2, p3)):
        out[(ids[0] - k) & 3] = piece[...].reshape(16, 16, 512)


def unpack_body(ids, mine, theirs, out, whole, sem):
    c = ids[1]
    for z in range(4):
        whole[:, core_rows(z, c), :] = mine[z]
        whole[:, core_rows(z, 1 - c), :] = theirs[z]
    to = move(whole, out, sem, 0)
    to.start()
    to.wait()


def unpack(ids, mine, theirs):
    return pl.pallas_call(
        unpack_body,
        out_shape=jax.ShapeDtypeStruct((16, 128, 512), BF16),
        in_specs=[SMEM, VMEM, VMEM],
        out_specs=HBM,
        scratch_shapes=[pltpu.VMEM((16, 128, 512), BF16), pltpu.SemaphoreType.DMA((1,))],
        compiler_params=pltpu.CompilerParams(vmem_limit_bytes=48 * MIB),
    )(ids, mine, theirs).reshape(2048, 512)


def pair_sum_body(ids, own, other, *outs):
    for k in range(4):
        at = band(ids[0] + k)
        outs[k][...] = (own[:, at, :] + other[:, at, :].astype(F32)).astype(BF16)


def part_sum_body(own, other, *outs):
    for k in range(3):
        at = slice(16 * k, 16 * k + 16)
        outs[k][...] = (own[at] + other[at].astype(F32)).astype(BF16)


def three_sum_body(ids, a, b, c, *outs):
    for k in range(4):
        at = band(ids[0] + k)
        total = a[:, at, :].astype(F32) + b[:, at, :].astype(F32) + c[:, at, :].astype(F32)
        outs[k][...] = total.astype(BF16)


def fetch_body(ids, meta, *rest):
    parts, (out, tab, picked, sems) = rest[:8], rest[8:]
    x, y = ids[2], ids[3]
    for kx in range(4):
        for ky in range(4):
            at = (kx * 4 + ky) * 16
            tab[at : at + 16, :, :256] = parts[ky][kx]
            tab[at : at + 16, :, 256:] = parts[4 + kx][ky]

    def out_to(i):
        return move(picked.at[i], out.at[i], sems, i)

    def owner(i, _):
        for e in range(32):
            slot = meta[i * 64 + e]
            kx = (x - (slot >> 6)) & 3
            ky = (y - ((slot >> 4) & 3)) & 3
            picked[i, e] = tab[(kx * 4 + ky) * 16 + (slot & 15)]
        out_to(i).start()
        return 0

    lax.fori_loop(0, 8, owner, 0)
    for i in range(8):
        out_to(i).wait()


def fetch(ids, meta, parts):
    return pl.pallas_call(
        fetch_body,
        out_shape=jax.ShapeDtypeStruct((8, 32, 16, 512), BF16),
        in_specs=[SMEM, SMEM] + [VMEM] * 8,
        out_specs=HBM,
        scratch_shapes=[
            pltpu.VMEM((256, 16, 512), BF16),
            pltpu.VMEM((8, 32, 16, 512), BF16),
            pltpu.SemaphoreType.DMA((8,)),
        ],
        compiler_params=pltpu.CompilerParams(vmem_limit_bytes=48 * MIB),
    )(ids, meta, *parts)


def grid_body(source, w_send, mask, pieces, out, w, m, p, acc, wide, o, s_w, s_m, s_p, s_out):
    def m_in(i):
        return move(mask.at[pl.ds(i * 8, 8)], m.at[pl.ds(i * 8, 8)], s_m, i)

    def p_in(i):
        return move(pieces.at[:, pl.ds(i * 8, 8)], p.at[:, pl.ds(i * 8, 8)], s_p, i)

    def out_to(i):
        at = pl.ds(pl.multiple_of(i * 512, 512), 512)
        return move(o.at[at, :], out.at[at, :], s_out, i)

    w_in = move(w_send, w, s_w, 0)
    for i in range(4):
        p_in(i).start()
        m_in(i).start()
    w_in.start()
    acc[...] = jnp.zeros_like(acc)

    def edges(i, _):
        p_in(i).wait()
        m_in(i).wait()
        for k in range(8):
            e = i * 8 + k
            for n in range(8):
                wide[k, 16 * n : 16 * n + 16, :] = p[n, e]
        for k in range(8):
            e = i * 8 + k
            at = pl.ds(pl.multiple_of(source[e] * 128, 128), 128)
            acc[at, :] += dot(m[e].astype(F32).astype(BF16), wide[k])
        return 0

    lax.fori_loop(0, 4, edges, 0)
    w_in.wait()

    def rows(i, _):
        at = pl.ds(pl.multiple_of(i * 512, 512), 512)
        o[at, :] = dot_t(acc[at, :].astype(BF16), w[...]).astype(BF16)
        out_to(i).start()
        return 0

    lax.fori_loop(0, 6, rows, 0)
    for i in range(6):
        out_to(i).wait()


def grid_gradient(source, w_send, mask, pieces):
    sems = lambda n: pltpu.SemaphoreType.DMA((n,))
    return pl.pallas_call(
        grid_body,
        out_shape=jax.ShapeDtypeStruct((3072, 512), BF16),
        in_specs=[SMEM, HBM, HBM, HBM],
        out_specs=HBM,
        scratch_shapes=[
            pltpu.VMEM((512, 512), BF16),
            pltpu.VMEM((32, 128, 128), jnp.int32),
            pltpu.VMEM((8, 32, 16, 512), BF16),
            pltpu.VMEM((3072, 512), F32),
            pltpu.VMEM((8, 128, 512), BF16),
            pltpu.VMEM((3072, 512), BF16),
            sems(1),
            sems(4),
            sems(4),
            sems(6),
        ],
        compiler_params=pltpu.CompilerParams(vmem_limit_bytes=56 * MIB),
    )(source, w_send, mask, pieces)


def column_exchange(pieces):
    return lax.all_to_all(pieces, "grid", 0, 0, tiled=True)


def own_rows(array, g):
    return lax.dynamic_index_in_dim(array.reshape(16, 8, 16, 512), g, 1, False).reshape(256, 512)


def per_device(
    grid_latent,
    mesh_latent,
    mesh_cotangent,
    w_send,
    w_self_enc,
    w_agg_enc,
    w_out_enc,
    w_pass,
    w_self_proc,
    w_agg_proc,
    w_out_proc,
    enc_source,
    enc_part,
    enc_block,
    enc_mask,
    proc_source,
    proc_target,
    proc_mask,
):
    messages, proc_mask = send_messages(enc_source, grid_latent, w_send, enc_mask, proc_mask)
    places = (lax.axis_index("grid"), lax.axis_index("mesh"))
    edges = (enc_part, enc_block, proc_source, proc_target)
    messages, (g, p), edges, mesh_latent, mesh_cotangent = lax.optimization_barrier(
        (messages, places, edges, mesh_latent, mesh_cotangent)
    )
    z, c = g // 2, g % 2
    ids = jnp.stack([z, c, p // 4, p % 4]).astype(jnp.int32)
    labels = jnp.concatenate([edges[0][:, 0] * 16 + edges[1], edges[2], edges[3]])
    arrived = column_exchange(messages)
    rows = own_rows(mesh_latent, g)
    cotangent = own_rows(mesh_cotangent, g)
    pre_self = dot(rows, w_self_enc)
    g_hid_proc = dot_t(cotangent, w_out_proc).astype(BF16)
    labels, pre_self, g_hid_proc, rows, cotangent = lax.optimization_barrier(
        (labels, pre_self, g_hid_proc, rows, cotangent)
    )
    meta = lax.all_gather(labels, "grid", axis=0, tiled=True)
    arrived, meta, proc_mask = lax.optimization_barrier((arrived, meta, proc_mask))
    by_y, by_x = combine(ids, meta, arrived)
    proc_mask, kept = lax.optimization_barrier((proc_mask, by_y[0]))
    masks = spread_z([proc_mask] * 4)
    summed = reduce_halves([kept, *by_y[1:]], by_x)
    pre_self, masks = lax.optimization_barrier((pre_self, tuple(masks)))
    pre_enc, first, *passed = local(
        enc_mlp_body,
        [ROWS32, ROWS] + [PIECE] * 4,
        [ids, *summed, pre_self, rows, w_agg_enc, w_out_enc, w_pass],
        scratch=[WIDE],
    )

    own = table(ids, spread_z(passed))
    tables = [over_mesh(own, 1), own, over_mesh(own, -1)]
    both = []
    for one in tables:
        both += [one, over_column(one, 0, 1)]
    mine, theirs = local(
        proc_body,
        [((16, 64, 128), F32), ((16, 64, 128), BF16)],
        [ids, meta, *masks, *both],
        smem=2,
        scratch=[pltpu.VMEM((48, 128, 128), BF16), pltpu.VMEM((16, 128, 128), F32)],
    )
    summed = local(pair_sum_body, [PIECE] * 4, [ids, mine, over_column(theirs, 0, 1)])
    pre_self_proc = dot(first, w_self_proc)
    out_rows, g_pre_proc, *g_agg = local(
        proc_mlp_body,
        [ROWS, ROWS] + [PIECE] * 4,
        [ids, *spread_z(summed), pre_self_proc, first, g_hid_proc, w_agg_proc, w_out_proc],
        scratch=[WIDE],
    )
    g_first_part = cotangent.astype(F32) + dot_t(g_pre_proc, w_self_proc)
    own = table(ids, spread_z(g_agg))
    mine, theirs = local(
        proc_back_body,
        [((48, 64, 128), F32), ((48, 64, 128), BF16)],
        [ids, meta, *masks, own, over_column(own, 0, 1)],
        smem=2,
        scratch=[pltpu.VMEM((16, 128, 128), BF16), pltpu.VMEM((48, 128, 128), F32)],
    )
    parts = local(part_sum_body, [((16, 64, 128), BF16)] * 3, [mine, over_column(theirs, 0, 1)], smem=0)
    out_rows, middle = lax.optimization_barrier((out_rows, parts[1]))
    parts = [parts[0], middle, parts[2]]
    out_parts = spread_z([out_rows] * 4)
    g_first_part, out_parts = lax.optimization_barrier((g_first_part, tuple(out_parts)))
    g_pass = local(
        three_sum_body, [PIECE] * 4, [ids, over_mesh(parts[0], -1), parts[1], over_mesh(parts[2], 1)]
    )
    left, right = local(
        enc_back_body,
        [((16, 16, 256), BF16)] * 2,
        [ids, *spread_z(g_pass), g_first_part, pre_enc, w_pass, w_out_enc, w_agg_enc],
        scratch=[WIDE],
    )

    packed = local(pack_body, [((4, 16, 16, 512), BF16)], [ids, *out_parts])[0]
    returned = column_exchange(fetch(ids, meta, gather_halves(left, right)))
    mesh_out = unpack(ids, packed, over_column(packed, 0, 1))
    returned, mesh_out = lax.optimization_barrier((returned, mesh_out))
    grid_grad = grid_gradient(enc_source, w_send, enc_mask, returned)
    return (mesh_out, grid_grad)


def solution(mesh):
    return jax.shard_map(
        per_device,
        mesh=mesh,
        in_specs=(
            P(("grid", "mesh"), None),
            P("mesh", None),
            P("mesh", None),
            P(),
            P(),
            P(),
            P(),
            P(),
            P(),
            P(),
            P(),
            P(("grid", "mesh")),
            P(("grid", "mesh"), None),
            P(("grid", "mesh")),
            P(("grid", "mesh"), None, None),
            P(("grid", "mesh")),
            P(("grid", "mesh")),
            P(("grid", "mesh"), None, None),
        ),
        out_specs=(P("mesh", None), P(("grid", "mesh"), None)),
        check_vma=False,
    )
```

```python
import functools

import jax
import jax.numpy as jnp
from jax import lax
from jax.experimental import pallas as pl
from jax.experimental.pallas import tpu as pltpu
from jax.sharding import PartitionSpec as P

BF16 = jnp.bfloat16
F32 = jnp.float32
MIB = 1024 * 1024
SMEM = pl.BlockSpec(memory_space=pltpu.SMEM)
VMEM = pl.BlockSpec(memory_space=pltpu.VMEM)
HBM = pl.BlockSpec(memory_space=pltpu.HBM)


def over_z(array, by):
    return lax.ppermute(array, "grid", [(2 * z + c, 2 * ((z + by) % 4) + c) for z in range(4) for c in range(2)])


def over_column(array, dz, dc):
    return lax.ppermute(
        array, "grid", [(2 * z + c, 2 * ((z + dz) % 4) + (c ^ dc)) for z in range(4) for c in range(2)]
    )


def over_x(array, by):
    return lax.ppermute(array, "mesh", [(4 * x + y, 4 * ((x + by) % 4) + y) for x in range(4) for y in range(4)])


def over_y(array, by):
    return lax.ppermute(array, "mesh", [(4 * x + y, 4 * x + (y + by) % 4) for x in range(4) for y in range(4)])


def over_mesh(array, by):
    return lax.ppermute(array, "mesh", [(p, (p + by) % 16) for p in range(16)])


def local(body, outs, ins, smem=1, scratch=(), limit=12):
    return pl.pallas_call(
        body,
        out_shape=[jax.ShapeDtypeStruct(shape, dtype) for shape, dtype in outs],
        in_specs=[SMEM] * smem + [VMEM] * (len(ins) - smem),
        out_specs=[VMEM] * len(outs),
        scratch_shapes=list(scratch),
        compiler_params=pltpu.CompilerParams(vmem_limit_bytes=limit * MIB),
    )(*ins)


def lanes(index):
    return pl.ds(pl.multiple_of((index & 3) * 128, 128), 128)


def dot(a, b):
    return jnp.dot(a, b, preferred_element_type=F32)


def dot_t(a, b):
    return lax.dot_general(a, b, (((1,), (1,)), ((), ())), preferred_element_type=F32)


def silu_slope(values):
    sigmoid_v = jax.nn.sigmoid(values)
    return sigmoid_v * (1.0 + values * (1.0 - sigmoid_v))


def move(source, target, sems, i):
    return pltpu.make_async_copy(source, target, sems.at[i])


def messages_body(
    source, latent, w_send, mask, other, out, other_out, x, w, m, o, sent, msg, o_b, s_x, s_w, s_m, s_o, s_out
):
    def x_in(i):
        at = pl.ds(pl.multiple_of(i * 512, 512), 512)
        return move(latent.at[at, :], x.at[at, :], s_x, i)

    def m_in(i):
        return move(mask.at[pl.ds(i * 8, 8)], m.at[pl.ds(i * 8, 8)], s_m, i)

    def out_to(i):
        return move(msg.at[:, pl.ds(i * 8, 8)], out.at[:, pl.ds(i * 8, 8)], s_out, i)

    w_in, o_in, o_to = move(w_send, w, s_w, 0), move(other, o, s_o, 0), move(o_b, other_out, s_o, 1)
    w_in.start()
    for i in range(6):
        x_in(i).start()
    for i in range(4):
        m_in(i).start()
    o_in.start()
    w_in.wait()

    def rows(i, _):
        x_in(i).wait()
        at = pl.ds(pl.multiple_of(i * 512, 512), 512)
        sent[at, :] = dot(x[at, :], w[...]).astype(BF16)
        return 0

    lax.fori_loop(0, 6, rows, 0)

    def edges(i, _):
        m_in(i).wait()
        for k in range(8):
            e = i * 8 + k
            block = sent[pl.ds(pl.multiple_of(source[e] * 128, 128), 128), :]
            message = lax.dot_general(
                m[e].astype(F32).astype(BF16), block, (((0,), (0,)), ((), ())), preferred_element_type=F32
            ).astype(BF16)
            for n in range(8):
                msg[n, e] = message[16 * n : 16 * n + 16, :]
        out_to(i).start()
        return 0

    lax.fori_loop(0, 4, edges, 0)
    o_in.wait()
    o_b[...] = o[...].astype(F32).astype(BF16)
    o_to.start()
    for i in range(4):
        out_to(i).wait()
    o_to.wait()


def send_messages(source, latent, w_send, mask, other):
    sems = lambda n: pltpu.SemaphoreType.DMA((n,))
    return pl.pallas_call(
        messages_body,
        out_shape=[
            jax.ShapeDtypeStruct((8, 32, 16, 512), BF16),
            jax.ShapeDtypeStruct((16, 128, 128), BF16),
        ],
        in_specs=[SMEM, HBM, HBM, HBM, HBM],
        out_specs=[HBM, HBM],
        scratch_shapes=[
            pltpu.VMEM((3072, 512), BF16),
            pltpu.VMEM((512, 512), BF16),
            pltpu.VMEM((32, 128, 128), jnp.int32),
            pltpu.VMEM((16, 128, 128), jnp.int32),
            pltpu.VMEM((3072, 512), BF16),
            pltpu.VMEM((8, 32, 16, 512), BF16),
            pltpu.VMEM((16, 128, 128), BF16),
            sems(6),
            sems(1),
            sems(4),
            sems(2),
            sems(4),
        ],
        compiler_params=pltpu.CompilerParams(vmem_limit_bytes=56 * MIB),
    )(source, latent, w_send, mask, other)


def combine_body(ids, meta, arrived, *rest):
    outs, acc = rest[:10], rest[10]
    x, y = ids[2], ids[3]
    acc[...] = jnp.zeros_like(acc)

    def add(n, _):
        acc[meta[(n >> 5) * 64 + (n & 31)]] += arrived[n].astype(F32)
        return 0

    lax.fori_loop(0, 256, add, 0, unroll=4)
    for kx in range(4):
        for ky in range(4):
            at = pl.ds((4 * ((x + kx) & 3) + ((y + ky) & 3)) * 16, 16)
            place(outs[:5], ky, kx, acc[at, :, :256].astype(BF16))
            place(outs[5:], kx, ky, acc[at, :, 256:].astype(BF16))


def place(refs, step, other, value):
    if step == 2:
        refs[2 + other // 2][other % 2] = value
    else:
        refs[{0: 0, 1: 1, 3: 4}[step]][other] = value


PARTS = [((4, 16, 16, 256), BF16)] * 2 + [((2, 16, 16, 256), BF16)] * 2 + [((4, 16, 16, 256), BF16)]
SMALL = [((16, 16, 256), BF16)] * 4


def combine(ids, meta, arrived):
    outs = local(
        combine_body,
        PARTS * 2,
        [ids, meta, arrived.reshape(256, 16, 512)],
        smem=2,
        scratch=[pltpu.VMEM((256, 16, 512), F32)],
        limit=20,
    )
    return outs[:5], outs[5:]


def relay_body(*refs):
    for q in range(2):
        on, back, from_back, from_on = refs[4 * q : 4 * q + 4]
        new_on, new_back = refs[8 + 2 * q : 10 + 2 * q]
        half = on.shape[0] // 2
        new_on[:half] = (on[:half].astype(F32) + from_back[...].astype(F32)).astype(BF16)
        new_on[half:] = on[half:]
        new_back[:half] = back[:half]
        new_back[half:] = (back[half:].astype(F32) + from_on[...].astype(F32)).astype(BF16)


def relay(first, first_over, second, second_over):
    ins = []
    for parts, over in ((first, first_over), (second, second_over)):
        ins += [parts[1], parts[4], over(parts[2], 1), over(parts[3], 3)]
    kind = (ins[0].shape, BF16)
    on_1, back_1, on_2, back_2 = local(relay_body, [kind] * 4, ins, smem=0)
    return (
        [first[0], first_over(on_1, 1), first_over(back_1, 3)],
        [second[0], second_over(on_2, 1), second_over(back_2, 3)],
    )


def add_rows_body(*refs):
    for q in range(2):
        a, b, c = refs[3 * q : 3 * q + 3]
        outs = refs[6 + 4 * q : 10 + 4 * q]
        for j in range(4):
            outs[j][...] = (a[j].astype(F32) + b[j].astype(F32) + c[j].astype(F32)).astype(BF16)


def reduce_halves(by_y, by_x):
    by_y, by_x = relay(by_y, over_y, by_x, over_x)
    sums = local(add_rows_body, SMALL * 2, [*by_y, *by_x], smem=0)
    left = [sums[0]] + [over_x(sums[k], k) for k in (1, 2, 3)]
    right = [sums[4]] + [over_y(sums[4 + k], k) for k in (1, 2, 3)]
    return [*left, *right]


def to_rows(z, pieces, wide):
    for k in range(4):
        wide[:, lanes(z - k)] = pieces[k][...].reshape(256, 128)
    return wide[...]


def from_rows(z, wide, outs):
    for k in range(4):
        outs[k][...] = wide[:, lanes(z + k)].reshape(16, 16, 128)


def enc_mlp_body(ids, *rest):
    terms, (pre_self, rows, w_agg, w_out, w_pass, pre_ref, first_ref) = rest[:8], rest[8:15]
    outs, wide = rest[15:19], rest[19]
    z = ids[0]
    pre = pre_self[...]
    for q in range(2):
        total = terms[4 * q][...].astype(F32)
        for more in terms[4 * q + 1 : 4 * q + 4]:
            total += more[...].astype(F32)
        pre += dot(total.astype(BF16).reshape(256, 256), w_agg[256 * q : 256 * q + 256, :])
    pre_ref[...] = pre
    hidden = jax.nn.silu(pre).astype(BF16)
    first = (rows[...].astype(F32) + dot(hidden, w_out[...])).astype(BF16)
    first_ref[...] = first
    wide[...] = dot(first, w_pass[...]).astype(BF16)
    from_rows(z, wide, outs)


def proc_mlp_body(ids, p0, p1, p2, p3, pre_self, rows, g_hidden, w_agg, w_out, out_ref, g_pre_ref, *rest):
    outs, wide = rest[:4], rest[4]
    z = ids[0]
    summed = to_rows(z, (p0, p1, p2, p3), wide)
    pre = pre_self[...] + dot(summed, w_agg[...])
    g_pre = (g_hidden[...].astype(F32) * silu_slope(pre)).astype(BF16)
    g_pre_ref[...] = g_pre
    wide[...] = dot_t(g_pre, w_agg[...]).astype(BF16)
    from_rows(z, wide, outs)
    hidden = jax.nn.silu(pre).astype(BF16)
    out_ref[...] = (rows[...].astype(F32) + dot(hidden, w_out[...])).astype(BF16)


def enc_back_body(ids, p0, p1, p2, p3, g_part, pre, w_pass, w_out, w_agg, left, right, wide):
    z = ids[0]
    g_pass = to_rows(z, (p0, p1, p2, p3), wide)
    g_first = (g_part[...] + dot_t(g_pass, w_pass[...])).astype(BF16)
    g_hidden = dot_t(g_first, w_out[...]).astype(BF16)
    g_pre = (g_hidden.astype(F32) * silu_slope(pre[...])).astype(BF16)
    g_agg = dot_t(g_pre, w_agg[...]).astype(BF16)
    left[...] = g_agg[:, :256].reshape(16, 16, 256)
    right[...] = g_agg[:, 256:].reshape(16, 16, 256)


ROWS = ((256, 512), BF16)
ROWS32 = ((256, 512), F32)
PIECE = ((16, 16, 128), BF16)
WIDE = pltpu.VMEM((256, 512), BF16)


def band(z):
    return pl.ds(pl.multiple_of((z & 3) * 16, 16), 16)


def table_body(ids, p0, p1, p2, p3, out):
    for k, piece in enumerate((p0, p1, p2, p3)):
        out[:, band(ids[0] - k), :] = piece[...]


def table(ids, pieces):
    return local(table_body, [((16, 64, 128), BF16)], [ids, *pieces])[0]


def stack_body(*refs):
    for k in range(4):
        refs[8][k] = refs[k][...]
        refs[9][k] = refs[4 + k][...]


def gather_halves(left, right):
    left = [left] + [over_x(left, k) for k in (1, 2, 3)]
    right = [right] + [over_y(right, k) for k in (1, 2, 3)]
    left, right = local(stack_body, [((4, 16, 16, 256), BF16)] * 2, [*left, *right], smem=0)
    return [left] + [over_y(left, k) for k in (1, 2, 3)] + [right] + [over_x(right, k) for k in (1, 2, 3)]


def spread_z(pieces):
    return [pieces[0]] + [over_z(pieces[k], k) for k in (1, 2, 3)]


def edge_loop(z, c, meta, one):
    for k in range(4):
        row = (2 * ((z - k) & 3) + c) * 64

        def four(n, _):
            at = row + n * 4
            one(k, n * 4, [(meta[at + 32 + e], meta[at + 48 + e]) for e in range(4)])
            return 0

        lax.fori_loop(0, 4, four, 0)


def core_rows(z, c):
    return pl.ds(pl.multiple_of(32 * z + 16 * c, 16), 16)


def join_rows(c, mine, theirs, whole, first):
    blocks = mine.shape[0]
    for z in range(4):
        at = slice(16 * z, 16 * z + 16)
        whole[first : first + blocks, core_rows(z, c), :] = mine[:, at, :]
        whole[first : first + blocks, core_rows(z, 1 - c), :] = theirs[:, at, :]


def part_rows(c, whole, own, other):
    for z in range(4):
        at = slice(16 * z, 16 * z + 16)
        own[:, at, :] = whole[:, core_rows(z, c), :]
        other[:, at, :] = whole[:, core_rows(z, 1 - c), :].astype(BF16)


def proc_body(ids, meta, *rest):
    masks, tables, (own, other, ext, acc) = rest[:4], rest[4:10], rest[10:]
    z, c = ids[0], ids[1]
    for k in range(3):
        join_rows(c, tables[2 * k], tables[2 * k + 1], ext, 16 * k)
    acc[...] = jnp.zeros_like(acc)

    def one(k, base, edges):
        terms = [
            lax.dot_general(masks[k][base + e], ext[source], (((0,), (0,)), ((), ())), preferred_element_type=F32)
            for e, (source, _) in enumerate(edges)
        ]
        for term, (_, target) in zip(terms, edges):
            acc[target] += term

    edge_loop(z, c, meta, one)
    part_rows(c, acc, own, other)


def proc_back_body(ids, meta, *rest):
    masks, (mine, theirs, own, other, grads, acc) = rest[:4], rest[4:]
    z, c = ids[0], ids[1]
    join_rows(c, mine, theirs, grads, 0)
    acc[...] = jnp.zeros_like(acc)

    def one(k, base, edges):
        terms = [dot(masks[k][base + e], grads[target]) for e, (_, target) in enumerate(edges)]
        for term, (source, _) in zip(terms, edges):
            acc[source] += term

    edge_loop(z, c, meta, one)
    part_rows(c, acc, own, other)


def pack_body(ids, p0, p1, p2, p3, out):
    for k, piece in enumerate((p0, p1, p2, p3)):
        out[(ids[0] - k) & 3] = piece[...].reshape(16, 16, 512)


def unpack_body(ids, mine, theirs, out, whole, sem):
    c = ids[1]
    for z in range(4):
        whole[:, core_rows(z, c), :] = mine[z]
        whole[:, core_rows(z, 1 - c), :] = theirs[z]
    to = move(whole, out, sem, 0)
    to.start()
    to.wait()


def unpack(ids, mine, theirs):
    return pl.pallas_call(
        unpack_body,
        out_shape=jax.ShapeDtypeStruct((16, 128, 512), BF16),
        in_specs=[SMEM, VMEM, VMEM],
        out_specs=HBM,
        scratch_shapes=[pltpu.VMEM((16, 128, 512), BF16), pltpu.SemaphoreType.DMA((1,))],
        compiler_params=pltpu.CompilerParams(vmem_limit_bytes=48 * MIB),
    )(ids, mine, theirs).reshape(2048, 512)


def pair_sum_body(ids, own, other, *outs):
    for k in range(4):
        at = band(ids[0] + k)
        outs[k][...] = (own[:, at, :] + other[:, at, :].astype(F32)).astype(BF16)


def part_sum_body(own, other, *outs):
    for k in range(3):
        at = slice(16 * k, 16 * k + 16)
        outs[k][...] = (own[at] + other[at].astype(F32)).astype(BF16)


def three_sum_body(ids, a, b, c, *outs):
    for k in range(4):
        at = band(ids[0] + k)
        total = a[:, at, :].astype(F32) + b[:, at, :].astype(F32) + c[:, at, :].astype(F32)
        outs[k][...] = total.astype(BF16)


def fetch_body(ids, meta, *rest):
    parts, (out, tab, picked, sems) = rest[:8], rest[8:]
    x, y = ids[2], ids[3]
    for kx in range(4):
        for ky in range(4):
            at = (kx * 4 + ky) * 16
            tab[at : at + 16, :, :256] = parts[ky][kx]
            tab[at : at + 16, :, 256:] = parts[4 + kx][ky]

    def out_to(i):
        return move(picked.at[i], out.at[i], sems, i)

    def owner(i, _):
        for e in range(32):
            slot = meta[i * 64 + e]
            kx = (x - (slot >> 6)) & 3
            ky = (y - ((slot >> 4) & 3)) & 3
            picked[i, e] = tab[(kx * 4 + ky) * 16 + (slot & 15)]
        out_to(i).start()
        return 0

    lax.fori_loop(0, 8, owner, 0)
    for i in range(8):
        out_to(i).wait()


def fetch(ids, meta, parts):
    return pl.pallas_call(
        fetch_body,
        out_shape=jax.ShapeDtypeStruct((8, 32, 16, 512), BF16),
        in_specs=[SMEM, SMEM] + [VMEM] * 8,
        out_specs=HBM,
        scratch_shapes=[
            pltpu.VMEM((256, 16, 512), BF16),
            pltpu.VMEM((8, 32, 16, 512), BF16),
            pltpu.SemaphoreType.DMA((8,)),
        ],
        compiler_params=pltpu.CompilerParams(vmem_limit_bytes=48 * MIB),
    )(ids, meta, *parts)


def grid_body(source, w_send, mask, pieces, out, w, m, p, acc, wide, o, s_w, s_m, s_p, s_out):
    def m_in(i):
        return move(mask.at[pl.ds(i * 8, 8)], m.at[pl.ds(i * 8, 8)], s_m, i)

    def p_in(i):
        return move(pieces.at[:, pl.ds(i * 8, 8)], p.at[:, pl.ds(i * 8, 8)], s_p, i)

    def out_to(i):
        at = pl.ds(pl.multiple_of(i * 512, 512), 512)
        return move(o.at[at, :], out.at[at, :], s_out, i)

    w_in = move(w_send, w, s_w, 0)
    for i in range(4):
        p_in(i).start()
        m_in(i).start()
    w_in.start()
    acc[...] = jnp.zeros_like(acc)

    def edges(i, _):
        p_in(i).wait()
        m_in(i).wait()
        for k in range(8):
            e = i * 8 + k
            for n in range(8):
                wide[k, 16 * n : 16 * n + 16, :] = p[n, e]
        for k in range(8):
            e = i * 8 + k
            at = pl.ds(pl.multiple_of(source[e] * 128, 128), 128)
            acc[at, :] += dot(m[e].astype(F32).astype(BF16), wide[k])
        return 0

    lax.fori_loop(0, 4, edges, 0)
    w_in.wait()

    def rows(i, _):
        at = pl.ds(pl.multiple_of(i * 512, 512), 512)
        o[at, :] = dot_t(acc[at, :].astype(BF16), w[...]).astype(BF16)
        out_to(i).start()
        return 0

    lax.fori_loop(0, 6, rows, 0)
    for i in range(6):
        out_to(i).wait()


def grid_gradient(source, w_send, mask, pieces):
    sems = lambda n: pltpu.SemaphoreType.DMA((n,))
    return pl.pallas_call(
        grid_body,
        out_shape=jax.ShapeDtypeStruct((3072, 512), BF16),
        in_specs=[SMEM, HBM, HBM, HBM],
        out_specs=HBM,
        scratch_shapes=[
            pltpu.VMEM((512, 512), BF16),
            pltpu.VMEM((32, 128, 128), jnp.int32),
            pltpu.VMEM((8, 32, 16, 512), BF16),
            pltpu.VMEM((3072, 512), F32),
            pltpu.VMEM((8, 128, 512), BF16),
            pltpu.VMEM((3072, 512), BF16),
            sems(1),
            sems(4),
            sems(4),
            sems(6),
        ],
        compiler_params=pltpu.CompilerParams(vmem_limit_bytes=56 * MIB),
    )(source, w_send, mask, pieces)


def column_exchange(pieces):
    return lax.all_to_all(pieces, "grid", 0, 0, tiled=True)


def own_rows(array, g):
    return lax.dynamic_index_in_dim(array.reshape(16, 8, 16, 512), g, 1, False).reshape(256, 512)


def per_device(
    grid_latent,
    mesh_latent,
    mesh_cotangent,
    w_send,
    w_self_enc,
    w_agg_enc,
    w_out_enc,
    w_pass,
    w_self_proc,
    w_agg_proc,
    w_out_proc,
    enc_source,
    enc_part,
    enc_block,
    enc_mask,
    proc_source,
    proc_target,
    proc_mask,
):
    messages, proc_mask = send_messages(enc_source, grid_latent, w_send, enc_mask, proc_mask)
    places = (lax.axis_index("grid"), lax.axis_index("mesh"))
    edges = (enc_part, enc_block, proc_source, proc_target)
    messages, (g, p), edges, mesh_latent, mesh_cotangent = lax.optimization_barrier(
        (messages, places, edges, mesh_latent, mesh_cotangent)
    )
    z, c = g // 2, g % 2
    ids = jnp.stack([z, c, p // 4, p % 4]).astype(jnp.int32)
    labels = jnp.concatenate([edges[0][:, 0] * 16 + edges[1], edges[2], edges[3]])
    arrived = column_exchange(messages)
    rows = own_rows(mesh_latent, g)
    cotangent = own_rows(mesh_cotangent, g)
    pre_self = dot(rows, w_self_enc)
    g_hid_proc = dot_t(cotangent, w_out_proc).astype(BF16)
    labels, pre_self, g_hid_proc, rows, cotangent = lax.optimization_barrier(
        (labels, pre_self, g_hid_proc, rows, cotangent)
    )
    meta = lax.all_gather(labels, "grid", axis=0, tiled=True)
    arrived, meta, proc_mask = lax.optimization_barrier((arrived, meta, proc_mask))
    by_y, by_x = combine(ids, meta, arrived)
    proc_mask, kept = lax.optimization_barrier((proc_mask, by_y[0]))
    masks = spread_z([proc_mask] * 4)
    summed = reduce_halves([kept, *by_y[1:]], by_x)
    pre_self, masks = lax.optimization_barrier((pre_self, tuple(masks)))
    pre_enc, first, *passed = local(
        enc_mlp_body,
        [ROWS32, ROWS] + [PIECE] * 4,
        [ids, *summed, pre_self, rows, w_agg_enc, w_out_enc, w_pass],
        scratch=[WIDE],
    )

    own = table(ids, spread_z(passed))
    tables = [over_mesh(own, 1), own, over_mesh(own, -1)]
    both = []
    for one in tables:
        both += [one, over_column(one, 0, 1)]
    mine, theirs = local(
        proc_body,
        [((16, 64, 128), F32), ((16, 64, 128), BF16)],
        [ids, meta, *masks, *both],
        smem=2,
        scratch=[pltpu.VMEM((48, 128, 128), BF16), pltpu.VMEM((16, 128, 128), F32)],
    )
    summed = local(pair_sum_body, [PIECE] * 4, [ids, mine, over_column(theirs, 0, 1)])
    pre_self_proc = dot(first, w_self_proc)
    out_rows, g_pre_proc, *g_agg = local(
        proc_mlp_body,
        [ROWS, ROWS] + [PIECE] * 4,
        [ids, *spread_z(summed), pre_self_proc, first, g_hid_proc, w_agg_proc, w_out_proc],
        scratch=[WIDE],
    )
    g_first_part = cotangent.astype(F32) + dot_t(g_pre_proc, w_self_proc)
    own = table(ids, spread_z(g_agg))
    mine, theirs = local(
        proc_back_body,
        [((48, 64, 128), F32), ((48, 64, 128), BF16)],
        [ids, meta, *masks, own, over_column(own, 0, 1)],
        smem=2,
        scratch=[pltpu.VMEM((16, 128, 128), BF16), pltpu.VMEM((48, 128, 128), F32)],
    )
    parts = local(part_sum_body, [((16, 64, 128), BF16)] * 3, [mine, over_column(theirs, 0, 1)], smem=0)
    out_rows, middle = lax.optimization_barrier((out_rows, parts[1]))
    parts = [parts[0], middle, parts[2]]
    out_parts = spread_z([out_rows] * 4)
    g_first_part, out_parts = lax.optimization_barrier((g_first_part, tuple(out_parts)))
    g_pass = local(
        three_sum_body, [PIECE] * 4, [ids, over_mesh(parts[0], -1), parts[1], over_mesh(parts[2], 1)]
    )
    left, right = local(
        enc_back_body,
        [((16, 16, 256), BF16)] * 2,
        [ids, *spread_z(g_pass), g_first_part, pre_enc, w_pass, w_out_enc, w_agg_enc],
        scratch=[WIDE],
    )

    packed = local(pack_body, [((4, 16, 16, 512), BF16)], [ids, *out_parts])[0]
    returned = column_exchange(fetch(ids, meta, gather_halves(left, right)))
    mesh_out = unpack(ids, packed, over_column(packed, 0, 1))
    returned, mesh_out = lax.optimization_barrier((returned, mesh_out))
    grid_grad = grid_gradient(enc_source, w_send, enc_mask, returned)
    return (mesh_out, grid_grad)


def solution(mesh):
    return jax.shard_map(
        per_device,
        mesh=mesh,
        in_specs=(
            P(("grid", "mesh"), None),
            P("mesh", None),
            P("mesh", None),
            P(),
            P(),
            P(),
            P(),
            P(),
            P(),
            P(),
            P(),
            P(("grid", "mesh")),
            P(("grid", "mesh"), None),
            P(("grid", "mesh")),
            P(("grid", "mesh"), None, None),
            P(("grid", "mesh")),
            P(("grid", "mesh")),
            P(("grid", "mesh"), None, None),
        ),
        out_specs=(P("mesh", None), P(("grid", "mesh"), None)),
        check_vma=False,
    )
```
